256 devices in a mesh: front: 4 (over z_hi, core), row: 4 (over x), col: 16 (over y, z_lo).
Axes of the slice: x: 4, y: 4, z: 8 (z_hi: 2, z_lo: 4; z = z_hi * 4 + z_lo), core: 2. Of those that a mesh axis runs over, the one named last changes fastest.
Arguments:
- front_matrix: float32 [4, 4096, 4096], P('front', 'row', 'col'), may hold values from -1 to 6, as said below
- child_updates: float32 [4, 2, 2048, 2048], P('front', None, 'row', 'col'), may hold values from -2 to 1, as said below
- child_map: int32 [4, 2, 2048], P('front'), may hold values from 0 to 4095, as said below
Outputs:
- front_out: float32 [4, 4096, 4096], P('front', 'row', 'col')
The draws below stay inside these ranges and needn't reach their ends.
Inputs may be any that keep to these rules, and one draw needn't show every extreme that they name: `front_matrix`: each front's matrix is symmetric; once both of its children's update blocks are added, the front is positive definite with no eigenvalue under 0.5. `child_updates`: each update block is symmetric and negative semidefinite. `child_map`: the entries of one child's map are distinct. Each aligned block of 128 entries has at most 16 values in any aligned block of 256 parent indices and exactly 16 in some; each aligned block of 512 entries has at most 128 values in any aligned block of 1024 parent indices and exactly 128 in some. For whichever of the two blockings has fewer blocks, every such count equals its bound. Each aligned block of 256 parent indices receives exactly 128 entries of one child, and each aligned block of 1024 exactly 512.
All inputs are finite; a program needn't handle non-finite values.
Results may differ from the reference program's by a relative error of at most 0.0001.
Values sent between devices are 32-bit elements; how exact they have to be, the bound alone decides.
A program may use at most 64 MiB of HBM per device.

```python
import jax
import jax.numpy as jnp
from jax import lax

F = 4096
UC = 2048
PW = 256
PANELS = 1
FRONTS = 4
ELIMINATED_COLS = 256
FINE = 16
COARSE = 4


DIAG_LOW = 0.5


DIAG_HIGH = 1.0


CHILD_SCALE = 0.5


def factor_draw(key, shape):
    return jnp.clip(jax.random.normal(key, shape, jnp.float32), -4.0, 4.0)


def gram_matrix(factor):
    rank_count = factor.shape[-1]
    product = jnp.einsum('...ik,...jk->...ij', factor, factor, precision=lax.Precision.HIGHEST) / rank_count
    return 0.5 * (product + jnp.swapaxes(product, -1, -2))


def child_blocks(key):
    rank_count = UC
    factor = factor_draw(jax.random.fold_in(key, 23), (FRONTS, 2, UC, rank_count))
    return -CHILD_SCALE * gram_matrix(factor)


def one_map(key):
    keys = jax.random.split(key, 6)
    group = FINE // COARSE
    block = UC // FINE
    base = block // FINE
    fine_ids = jnp.arange(FINE, dtype=jnp.int32)
    coarse_perm = jax.random.permutation(keys[0], COARSE).astype(jnp.int32)

    def permute_group(one_key):
        return jax.random.permutation(one_key, group).astype(jnp.int32)

    def permute_block(one_key):
        return jax.random.permutation(one_key, block).astype(jnp.int32)

    def permute_spots(one_key):
        return jax.random.permutation(one_key, 2 * block).astype(jnp.int32)
    inner_perm = jax.vmap(permute_group)(jax.random.split(keys[1], COARSE))
    target = group * coarse_perm[fine_ids // group] + inner_perm[fine_ids // group, fine_ids % group]
    pair_shift = jax.random.randint(keys[2], (FINE // 2,), 1, base + 1, dtype=jnp.int32)
    forced = jax.random.randint(keys[3], (), 0, FINE // 2, dtype=jnp.int32)
    pair_shift = jnp.where(jnp.arange(FINE // 2, dtype=jnp.int32) == forced, base, pair_shift)
    shift = pair_shift[fine_ids // 2]
    partner_target = target[fine_ids ^ 1]
    counts = base + shift[:, None] * (fine_ids[None, :] == target[:, None]).astype(jnp.int32)
    counts = counts - shift[:, None] * (fine_ids[None, :] == partner_target[:, None]).astype(jnp.int32)
    inclusive = jnp.cumsum(counts, axis=1)
    begin = inclusive - counts
    offset = jnp.cumsum(counts, axis=0) - counts
    order_table = jax.vmap(permute_block)(jax.random.split(keys[4], FINE))
    ranked = order_table.reshape(-1)
    source_block = jnp.arange(UC, dtype=jnp.int32) // block
    dest = jnp.sum((inclusive[source_block] <= ranked[:, None]).astype(jnp.int32), axis=1)
    within = ranked - begin[source_block, dest]
    place = offset[source_block, dest] + within
    spots = jax.vmap(permute_spots)(jax.random.split(keys[5], FINE))[:, :block]
    return dest * (2 * block) + spots[dest, place]


def draw_child_map(key, part):
    keys = jax.random.split(jax.random.fold_in(key, 37), FRONTS * 2)
    return jax.vmap(one_map)(keys).reshape(FRONTS, 2, UC)


def draw_child_updates(key, part):
    return child_blocks(key)


def front_blocks(key, part):
    rank_count = F // 8
    factor = factor_draw(jax.random.fold_in(key, 11), (FRONTS, F, rank_count))
    key_diagonal = jax.random.fold_in(key, 13)
    diagonal = jax.random.uniform(key_diagonal, (FRONTS, F), jnp.float32, DIAG_LOW, DIAG_HIGH)
    updates = child_blocks(key)
    mappings = draw_child_map(key, part)
    on_diagonal = jnp.arange(F)[:, None] == jnp.arange(F)[None, :]
    fronts = []
    for front_index in range(FRONTS):
        partner = front_index ^ 1
        assembled_base = gram_matrix(factor[front_index]) + jnp.where(on_diagonal, diagonal[front_index][:, None], 0.0)
        own_map = mappings[front_index, 0]
        other_map = mappings[partner, 1]
        assembled_base = assembled_base.at[own_map[:, None], own_map[None, :]].add(-updates[front_index, 0])
        assembled_base = assembled_base.at[other_map[:, None], other_map[None, :]].add(-updates[partner, 1])
        fronts.append(assembled_base)
    return jnp.stack(fronts)


def draw_front_matrix(key, part):
    return front_blocks(key, part)


def setup_inputs(seed: int = 0) -> dict:
    seeds = jax.random.split(jax.random.key(seed), 4)
    return {
        "front_matrix": draw_front_matrix(jax.random.fold_in(seeds[3], 71), 0),
        "child_updates": draw_child_updates(jax.random.fold_in(seeds[3], 71), 0),
        "child_map": draw_child_map(jax.random.fold_in(seeds[3], 71), 0),
    }


def assemble(front_entries, update, mapping):
    return front_entries.at[mapping[:, None], mapping[None, :]].add(update)

def reference(front_matrix, child_updates, child_map):
    results = []
    all_rows = jnp.arange(F, dtype=jnp.int32)
    for front_index in range(FRONTS):
        partner = front_index ^ 1
        front_entries = front_matrix[front_index]
        front_entries = assemble(front_entries, child_updates[front_index, 0], child_map[front_index, 0])
        front_entries = assemble(front_entries, child_updates[partner, 1], child_map[partner, 1])
        stored_factor = []
        for panel_index in range(PANELS):
            first_column = panel_index * PW
            pivot = front_entries[first_column:first_column + PW, first_column:first_column + PW]
            factor = jnp.linalg.cholesky(pivot)
            column_part = front_entries[:, first_column:first_column + PW]
            solved = jax.scipy.linalg.solve_triangular(factor, column_part.T, lower=True).T
            solved = jnp.where(all_rows[:, None] < first_column, 0.0, solved)
            in_panel = (all_rows >= first_column) & (all_rows < first_column + PW)
            factor_rows = jnp.take(factor, jnp.clip(all_rows - first_column, 0, PW - 1), axis=0)
            solved = jnp.where(in_panel[:, None], factor_rows, solved)
            front_entries = front_entries - jnp.dot(solved.astype(jnp.float32), solved.T.astype(jnp.float32), precision=lax.Precision.HIGHEST, preferred_element_type=jnp.float32)
            stored_factor.append(solved)
        factored_front = front_entries.at[:, :ELIMINATED_COLS].set(jnp.concatenate(stored_factor, axis=1))
        factored_front = factored_front.at[:ELIMINATED_COLS, ELIMINATED_COLS:].set(0.0)
        results.append(factored_front)
    return jnp.stack(results)
```

```python
import functools

import jax
import jax.numpy as jnp
from jax import lax
from jax.experimental import pallas as pl
from jax.experimental.pallas import tpu as pltpu
from jax.sharding import PartitionSpec as P

PW = 256
ROWS = 4
COLS = 16
RB = 1024
CB = 256
UR = 512
UCB = 128
CAPR = 128
CAPC = 16
MESH = pl.DeviceIdType.MESH
F32 = jnp.float32
BF16 = jnp.bfloat16
VMEM_LIMIT = 48 * 1024 * 1024


def parts3(x):
    hi = x.astype(BF16)
    rest = x - hi.astype(F32)
    mid = rest.astype(BF16)
    low = (rest - mid.astype(F32)).astype(BF16)
    return hi, mid, low


def dot_nt(a, b):
    return lax.dot_general(a, b, (((1,), (1,)), ((), ())), preferred_element_type=F32)


def dot_nn(a, b):
    return lax.dot_general(a, b, (((1,), (0,)), ((), ())), preferred_element_type=F32)


def dot_tn(a, b):
    return lax.dot_general(a, b, (((0,), (0,)), ((), ())), preferred_element_type=F32)


def split2(x):
    hi = x.astype(BF16)
    return hi, (x - hi.astype(F32)).astype(BF16)


def dot3(dot, a, b):
    ah, al = split2(a)
    bh, bl = split2(b)
    return dot(ah, bh) + (dot(ah, bl) + dot(al, bh))


def iota(shape, dim):
    return lax.broadcasted_iota(jnp.int32, shape, dim)


def onehot(rows, index):
    return (iota((rows, index.shape[1]), 0) == index).astype(F32).astype(BF16)


def before(n):
    return (iota((n, n), 0) < iota((n, n), 1)).astype(F32).astype(BF16)


def ranked_slot(dest, groups, cap):
    hit = iota((groups, dest.shape[1]), 0) == dest
    hits = hit.astype(F32)
    count = dot_nn(hits.astype(BF16), before(dest.shape[1]))
    rank = jnp.sum(jnp.where(hit, count, 0.0), axis=0, keepdims=True)
    return dest * cap + rank.astype(jnp.int32)


def pack_kernel(pos, u0, u1, m_ref, x_ref):
    r = pos[0]
    c = pos[1]
    for k in range(2):
        u_ref = u0 if k == 0 else u1
        mr = m_ref[k : k + 1, pl.ds(pl.multiple_of(r * UR, UR), UR)]
        mc = m_ref[k : k + 1, pl.ds(pl.multiple_of(c * UCB, UCB), UCB)]
        rp = onehot(UR, ranked_slot(mr // RB, 8, CAPR))
        cp = onehot(COLS * CAPC, ranked_slot(mc // CB, COLS, CAPC))
        x = None
        for part in parts3(u_ref[...]):
            t = dot_nt(cp, part).astype(BF16)
            piece = dot_nt(t, rp)
            x = piece if x is None else x + piece
        for dst in range(ROWS):
            x_ref[dst * COLS : (dst + 1) * COLS, k] = x[:, dst * CAPR : (dst + 1) * CAPR].reshape(COLS, CAPC, CAPR)


def exchange_kernel(x_ref, y_ref, send_sem, recv_sem, local_sem):
    r = lax.axis_index("row")
    c = lax.axis_index("col")
    me = r * COLS + c
    n = ROWS * COLS
    barrier = pltpu.get_barrier_semaphore()

    def greet(o, _):
        t = lax.rem(me + o, n)
        pl.semaphore_signal(
            barrier, inc=1, device_id={"row": t // COLS, "col": t % COLS}, device_id_type=MESH
        )
        return 0

    lax.fori_loop(1, n, greet, 0)
    pl.semaphore_wait(barrier, n - 1)

    def send(o, _):
        t = lax.rem(me + o, n)
        tr = t // COLS
        tc = t % COLS
        pltpu.make_async_remote_copy(
            src_ref=x_ref.at[t],
            dst_ref=y_ref.at[me],
            send_sem=send_sem,
            recv_sem=recv_sem,
            device_id={"row": tr, "col": tc},
            device_id_type=MESH,
        ).start()
        return 0

    lax.fori_loop(1, n, send, 0)
    own = pltpu.make_async_copy(x_ref.at[me], y_ref.at[me], local_sem)
    own.start()
    own.wait()

    every = pltpu.make_async_remote_copy(
        src_ref=x_ref.at[pl.ds(0, n - 1)],
        dst_ref=y_ref.at[pl.ds(0, n - 1)],
        send_sem=send_sem,
        recv_sem=recv_sem,
        device_id={"row": lax.rem(r + 1, ROWS), "col": c},
        device_id_type=MESH,
    )
    every.wait_recv()
    every.wait_send()


def unpack_kernel(pos, y_ref, m_ref, m16_ref, f_ref, a_ref, top_ref):
    r = pos[0]
    c = pos[1]
    mi = jnp.concatenate(
        [m_ref[k : k + 1, s * UR : (s + 1) * UR] for k in range(2) for s in range(ROWS)], axis=0
    )
    hit = (mi // RB) == r
    rank = dot_nn(hit.astype(F32).astype(BF16), before(UR)).astype(jnp.int32)
    slot = jnp.where(hit, rank, -1)
    mj = m16_ref[...]
    hit16 = (mj // CB) == c
    rank16 = dot_nn(hit16.astype(F32).astype(BF16), before(UCB)).astype(jnp.int32)
    slot16 = jnp.where(hit16, rank16 + CAPC * (iota((2 * COLS, UCB), 0) % COLS), -1)
    total = f_ref[...]
    eight = iota((8, 1), 0)
    for k in range(2):
        pieces = []
        for s in range(ROWS):
            row = k * ROWS + s
            g = onehot(CAPR, slot[row : row + 1, :])
            v = mi[row : row + 1, :] % RB
            vals = jnp.where(eight == 0, v // 256, v % 256).astype(F32).astype(BF16)
            got = dot_nt(vals, g)
            pieces.append(got[0:1, :] * 256.0 + got[1:2, :])
        rloc = jnp.concatenate(pieces, axis=1).astype(jnp.int32)
        tslot = jnp.concatenate([slot16[k * COLS + s : k * COLS + s + 1, :] for s in range(COLS)], axis=1)
        g = onehot(COLS * CAPC, tslot)
        v = (m_ref[k : k + 1, :] % CB).astype(F32).astype(BF16)
        got = dot_nt(jnp.broadcast_to(v, (8, COLS * UCB)), g)
        qloc = got[0:1, :].astype(jnp.int32)
        rpl = onehot(RB, rloc)
        cpl = onehot(CB, qloc)
        y = jnp.concatenate(
            [y_ref[s * COLS : (s + 1) * COLS, k].reshape(COLS * CAPC, CAPR) for s in range(ROWS)], axis=1
        )
        for part in parts3(y):
            w = dot_nn(cpl, part).astype(BF16)
            total = total + dot_nt(rpl, w)
    a_ref[...] = total
    top_ref[...] = total[:PW, :]


def spread_kernel(top_ref, xb_ref, pr_ref, pv_ref, s_sem, r_sem, l_sem):
    r = lax.axis_index("row")
    c = lax.axis_index("col")
    y = c // 4
    z = c % 4
    barrier = pltpu.get_barrier_semaphore()
    for o in range(1, 4):
        for target in (
            {"row": (r + o) % 4, "col": c},
            {"row": r, "col": ((y + o) % 4) * 4 + z},
            {"row": r, "col": y * 4 + (z + o) % 4},
        ):
            pl.semaphore_signal(barrier, inc=1, device_id=target, device_id_type=MESH)
    pl.semaphore_wait(barrier, 9)

    def remote(src, dst, i, j, target):
        return pltpu.make_async_remote_copy(
            src_ref=src, dst_ref=dst, send_sem=s_sem.at[i], recv_sem=r_sem.at[j],
            device_id=target, device_id_type=MESH,
        )

    @pl.when(r == 0)
    def _():
        for o in range(1, 4):
            remote(top_ref, xb_ref, o - 1, 0, {"row": (r + o) % 4, "col": c}).start()
        cp = pltpu.make_async_copy(top_ref, xb_ref, l_sem)
        cp.start()
        cp.wait()

    @pl.when(r != 0)
    def _():
        remote(top_ref, xb_ref, 0, 0, {"row": 0, "col": c}).wait_recv()

    @pl.when(c == 0)
    def _():
        for o in range(1, 4):
            remote(xb_ref, pv_ref, 2 + o, 1, {"row": r, "col": o * 4}).start()
        cp = pltpu.make_async_copy(xb_ref, pv_ref, l_sem)
        cp.start()
        cp.wait()

    @pl.when(y == r)
    def _():
        for o in range(1, 4):
            remote(xb_ref, pr_ref.at[z], 5 + o, 2, {"row": r, "col": ((y + o) % 4) * 4 + z}).start()
        cp = pltpu.make_async_copy(xb_ref, pr_ref.at[z], l_sem)
        cp.start()
        cp.wait()

    @pl.when(z == 0)
    def _():
        @pl.when(y != 0)
        def _():
            remote(xb_ref, pv_ref, 0, 1, {"row": r, "col": 0}).wait_recv()

        for o in range(1, 4):
            remote(pv_ref, pv_ref, 8 + o, 1, {"row": r, "col": y * 4 + o}).start()

    @pl.when(y != r)
    def _():
        remote(xb_ref, pr_ref.at[z], 0, 2, {"row": r, "col": r * 4 + z}).wait_recv()

    for o in range(1, 4):
        remote(
            pr_ref.at[z], pr_ref.at[z], 11 + o, 2 + o, {"row": r, "col": y * 4 + (z + o) % 4}
        ).start()

    @pl.when(z != 0)
    def _():
        remote(pv_ref, pv_ref, 0, 1, {"row": r, "col": y * 4}).wait_recv()

    for o in range(1, 4):
        remote(pr_ref.at[z], pr_ref.at[(z - o) % 4], 0, 2 + o, {"row": r, "col": c}).wait_recv()

    @pl.when(r == 0)
    def _():
        for o in range(1, 4):
            remote(top_ref, xb_ref, o - 1, 0, {"row": 1, "col": c}).wait_send()

    @pl.when(c == 0)
    def _():
        for o in range(1, 4):
            remote(xb_ref, pv_ref, 2 + o, 1, {"row": r, "col": 4}).wait_send()

    @pl.when(y == r)
    def _():
        for o in range(1, 4):
            remote(xb_ref, pr_ref.at[z], 5 + o, 2, {"row": r, "col": 4}).wait_send()

    @pl.when(z == 0)
    def _():
        for o in range(1, 4):
            remote(pv_ref, pv_ref, 8 + o, 1, {"row": r, "col": 1}).wait_send()

    for o in range(1, 4):
        remote(pr_ref.at[z], pr_ref.at[z], 11 + o, 2 + o, {"row": r, "col": 1}).wait_send()


NB = 8


def factorize(pv_ref, m_ref):
    n = PW
    m_ref[:, :n] = pv_ref[...]
    m_ref[:, n:] = (iota((n, n), 0) == iota((n, n), 1)).astype(F32)
    sub = iota((NB, 1), 0)
    for b in range(0, n, NB):
        d = m_ref[b : b + NB, (b // 128) * 128 : (b // 128) * 128 + 128]
        rows = m_ref[b : b + NB, :]
        at = b % 128
        for k in range(NB):
            col = d[:, at + k : at + k + 1]
            piv = lax.rsqrt(d[k : k + 1, at + k : at + k + 1])
            mul = jnp.where(sub > k, col * piv, 0.0)
            rk = rows[k : k + 1, :] * piv
            dk = d[k : k + 1, :] * piv
            rows = jnp.where(sub == k, rk, rows - mul * rk)
            d = jnp.where(sub == k, dk, d - mul * dk)
        rows = jnp.where(iota((NB, 2 * n), 1) < b + iota((NB, 2 * n), 0), 0.0, rows)
        m_ref[b : b + NB, :] = rows
        if b + NB < n:
            left = rows[:, :n]
            upd = lax.dot_general(
                left, rows, (((0,), (0,)), ((), ())), preferred_element_type=F32,
                precision=lax.Precision.HIGHEST,
            )
            m_ref[b + NB :, :] = m_ref[b + NB :, :] - upd[b + NB :, :]


def final_kernel(pos, a_ref, xb_ref, pr_ref, pv_ref, o_ref, m_ref):
    r = pos[0]
    c = pos[1]
    factorize(pv_ref, m_ref)
    inv = m_ref[:, PW:]

    @pl.when(c == 0)
    def _():
        for s in range(4):
            o_ref[s * 256 : (s + 1) * 256, :] = lax.dot_general(
                pr_ref[s], inv, (((0,), (1,)), ((), ())), preferred_element_type=F32,
                precision=lax.Precision.HIGHEST,
            )

        @pl.when(r == 0)
        def _():
            o_ref[:PW, :] = m_ref[:, :PW].T

    @pl.when(c != 0)
    def _():
        right = dot3(dot_nn, inv, xb_ref[...])
        for s in range(4):
            left = dot3(dot_nn, inv, pr_ref[s])
            o_ref[s * 256 : (s + 1) * 256, :] = a_ref[s * 256 : (s + 1) * 256, :] - dot3(
                dot_tn, left, right
            )

        @pl.when(r == 0)
        def _():
            o_ref[:PW, :] = jnp.zeros((PW, CB), F32)


def vm():
    return pl.BlockSpec(memory_space=pltpu.VMEM)


def sm():
    return pl.BlockSpec(memory_space=pltpu.SMEM)


def shape(*s):
    return jax.ShapeDtypeStruct(s, F32)


def local_params():
    return pltpu.CompilerParams(vmem_limit_bytes=VMEM_LIMIT)


def remote_params(i):
    return pltpu.CompilerParams(
        vmem_limit_bytes=VMEM_LIMIT, collective_id=i, has_side_effects=True
    )


def pack(pos, u0, u1, maps):
    return pl.pallas_call(
        pack_kernel,
        out_shape=shape(ROWS * COLS, 2, CAPC, CAPR),
        in_specs=[sm(), vm(), vm(), vm()],
        out_specs=vm(),
        compiler_params=local_params(),
    )(pos, u0, u1, maps)


def exchange(x):
    return pl.pallas_call(
        exchange_kernel,
        out_shape=shape(ROWS * COLS, 2, CAPC, CAPR),
        in_specs=[vm()],
        out_specs=vm(),
        scratch_shapes=[pltpu.SemaphoreType.DMA] * 3,
        compiler_params=remote_params(1),
    )(x)


def unpack(pos, y, maps, f):
    return pl.pallas_call(
        unpack_kernel,
        out_shape=[shape(RB, CB), shape(PW, CB)],
        in_specs=[sm(), vm(), vm(), vm(), vm()],
        out_specs=[vm(), vm()],
        compiler_params=local_params(),
    )(pos, y, maps, maps.reshape(2 * COLS, UCB), f)


def spread(top):
    return pl.pallas_call(
        spread_kernel,
        out_shape=[shape(PW, CB), shape(4, PW, CB), shape(PW, CB)],
        in_specs=[vm()],
        out_specs=[vm()] * 3,
        scratch_shapes=[
            pltpu.SemaphoreType.DMA((15,)),
            pltpu.SemaphoreType.DMA((6,)),
            pltpu.SemaphoreType.DMA,
        ],
        compiler_params=remote_params(2),
    )(top)


def final(pos, a, xb, pr, pv):
    return pl.pallas_call(
        final_kernel,
        out_shape=shape(RB, CB),
        in_specs=[sm(), vm(), vm(), vm(), vm()],
        out_specs=vm(),
        scratch_shapes=[pltpu.VMEM((PW, 2 * PW), F32)],
        compiler_params=local_params(),
    )(pos, a, xb, pr, pv)


def per_device(front_matrix, child_updates, child_map):
    pairs = [(s, s ^ 1) for s in range(4)]
    u1 = lax.ppermute(child_updates[0, 1], "front", pairs)
    m1 = lax.ppermute(child_map[0, 1], "front", pairs)
    maps = jnp.stack([child_map[0, 0], m1])
    pos = jnp.stack([lax.axis_index("row"), lax.axis_index("col")]).astype(jnp.int32)
    x = pack(pos, child_updates[0, 0], u1, maps)
    y = exchange(x)
    a, top = unpack(pos, y, maps, front_matrix[0])
    xb, pr, pv = spread(top)
    return final(pos, a, xb, pr, pv)[None]


def solution(mesh):
    in_specs = (P("front", "row", "col"), P("front", None, "row", "col"), P("front", None, None))
    return jax.shard_map(
        per_device, mesh=mesh, in_specs=in_specs, out_specs=P("front", "row", "col"), check_vma=False
    )
```

```python
import functools

import jax
import jax.numpy as jnp
from jax import lax
from jax.experimental import pallas as pl
from jax.experimental.pallas import tpu as pltpu
from jax.sharding import PartitionSpec as P

PW = 256
ROWS = 4
COLS = 16
RB = 1024
CB = 256
UR = 512
UCB = 128
CAPR = 128
CAPC = 16
CAPP = 64
OB = 64
MESH = pl.DeviceIdType.MESH
F32 = jnp.float32
BF16 = jnp.bfloat16
VMEM_LIMIT = 48 * 1024 * 1024


def parts3(x):
    hi = x.astype(BF16)
    rest = x - hi.astype(F32)
    mid = rest.astype(BF16)
    low = (rest - mid.astype(F32)).astype(BF16)
    return hi, mid, low


def dot_nt(a, b):
    return lax.dot_general(a, b, (((1,), (1,)), ((), ())), preferred_element_type=F32)


def dot_nn(a, b):
    return lax.dot_general(a, b, (((1,), (0,)), ((), ())), preferred_element_type=F32)


def dot_tn(a, b):
    return lax.dot_general(a, b, (((0,), (0,)), ((), ())), preferred_element_type=F32)


def split2(x):
    hi = x.astype(BF16)
    return hi, (x - hi.astype(F32)).astype(BF16)


def dot3(dot, a, b):
    ah, al = split2(a)
    bh, bl = split2(b)
    return dot(ah, bh) + (dot(ah, bl) + dot(al, bh))


def iota(shape, dim):
    return lax.broadcasted_iota(jnp.int32, shape, dim)


def onehot(rows, index):
    return (iota((rows, index.shape[1]), 0) == index).astype(F32).astype(BF16)


def before(n):
    return (iota((n, n), 0) < iota((n, n), 1)).astype(F32).astype(BF16)


def ranked_slot(dest, groups, cap):
    hit = iota((groups, dest.shape[1]), 0) == dest
    hits = hit.astype(F32)
    count = dot_nn(hits.astype(BF16), before(dest.shape[1]))
    rank = jnp.sum(jnp.where(hit, count, 0.0), axis=0, keepdims=True)
    return dest * cap + rank.astype(jnp.int32)


def pack_kernel(pos, u0, u1, m_ref, m16_ref, x_ref, xp_ref, idx_ref):
    r = pos[0]
    c = pos[1]
    panel = None
    for k in range(2):
        u_ref = u0 if k == 0 else u1
        mr = m_ref[k : k + 1, pl.ds(pl.multiple_of(r * UR, UR), UR)]
        mc = m_ref[k : k + 1, pl.ds(pl.multiple_of(c * UCB, UCB), UCB)]
        rp = onehot(UR, ranked_slot(mr // RB, 8, CAPR))
        cp = onehot(COLS * CAPC, ranked_slot(mc // CB, COLS, CAPC))
        first = mr < PW
        place = ranked_slot(jnp.where(first, 0, 1), 8, 0) + CAPP * k
        pp = onehot(2 * CAPP, jnp.where(first, place, -1))
        x = None
        for part in parts3(u_ref[...]):
            t = dot_nt(cp, part).astype(BF16)
            piece = dot_nt(t, rp)
            x = piece if x is None else x + piece
            piece = dot_nt(t, pp)
            panel = piece if panel is None else panel + piece
        for dst in range(ROWS):
            x_ref[dst * COLS : (dst + 1) * COLS, k] = x[
                :, dst * CAPR : (dst + 1) * CAPR
            ].reshape(COLS, CAPC, CAPR)
    xp_ref[...] = panel.reshape(COLS, CAPC, 2 * CAPP)

    mi = jnp.concatenate(
        [m_ref[k : k + 1, s * UR : (s + 1) * UR] for k in range(2) for s in range(ROWS)], axis=0
    )
    child = iota((8, UR), 0) // ROWS

    def slots(hit, base):
        rank = dot_nn(hit.astype(F32).astype(BF16), before(hit.shape[1])).astype(jnp.int32)
        return jnp.where(hit, rank + base, -1)

    slot = slots((mi // RB) == r, 0)
    pslot = slots(mi < PW, CAPP * child)
    mj = m16_ref[...]
    slot16 = slots((mj // CB) == c, CAPC * (iota((2 * COLS, UCB), 0) % COLS))
    eight = iota((8, 1), 0)
    for k in range(2):
        rows = []
        prows = []
        for s in range(ROWS):
            row = k * ROWS + s
            v = mi[row : row + 1, :]
            vals = jnp.where(eight == 0, (v % RB) // 256, v % 256).astype(F32).astype(BF16)
            got = dot_nt(vals, onehot(CAPR, slot[row : row + 1, :]))
            rows.append(got[0:1, :] * 256.0 + got[1:2, :])
            vals = jnp.broadcast_to((v % 256 + 1).astype(F32).astype(BF16), (8, UR))
            got = dot_nt(vals, onehot(2 * CAPP, pslot[row : row + 1, :]))
            prows.append(got[0:1, :] - 1.0)
        idx_ref[k : k + 1, :] = jnp.concatenate(rows, axis=1).astype(jnp.int32)
        idx_ref[2 + k : 3 + k, :] = jnp.concatenate(prows, axis=1).astype(jnp.int32)
        tslot = jnp.concatenate(
            [slot16[k * COLS + s : k * COLS + s + 1, :] for s in range(COLS)], axis=1
        )
        v = (m_ref[k : k + 1, :] % CB).astype(F32).astype(BF16)
        got = dot_nt(jnp.broadcast_to(v, (8, COLS * UCB)), onehot(COLS * CAPC, tslot))
        idx_ref[4 + k : 5 + k, :CB] = got[0:1, :].astype(jnp.int32)
        idx_ref[4 + k : 5 + k, CB:] = got[0:1, :].astype(jnp.int32)
    idx_ref[6:8, :] = jnp.zeros((2, UR), jnp.int32)


def move_kernel(
    x_ref, xp_ref, idx_ref, f_ref, y_ref, xb_ref, pr_ref, pv_ref, yp_ref,
    ft_ref, xs, xr, ps, prs, bs, br, qs, qr, ds, vs, vr, vt, fs,
):
    r = lax.axis_index("row")
    c = lax.axis_index("col")
    y = c // 4
    z = c % 4
    me = r * COLS + c
    n = ROWS * COLS
    barrier = pltpu.get_barrier_semaphore()

    def at(t):
        return {"row": t // COLS, "col": t % COLS}

    def greet(o, _):
        pl.semaphore_signal(barrier, inc=1, device_id=at(lax.rem(me + o, n)), device_id_type=MESH)
        return 0

    lax.fori_loop(1, n, greet, 0)
    pl.semaphore_wait(barrier, n - 1)

    def remote(src, dst, s_sem, r_sem, row, col):
        return pltpu.make_async_remote_copy(
            src_ref=src, dst_ref=dst, send_sem=s_sem, recv_sem=r_sem,
            device_id={"row": row, "col": col}, device_id_type=MESH,
        )

    def quarter(i):
        return pl.ds(pl.multiple_of(i * 64, 64), 64)

    def sixteenth(i):
        return pl.ds(pl.multiple_of(i * 16, 16), 16)

    top = pltpu.make_async_copy(f_ref.at[0:PW], ft_ref, fs)
    top.start()

    def send_panel(o, _):
        t = lax.rem(c + o, COLS)
        remote(xp_ref.at[t], yp_ref.at[me], ps, prs, 0, t).start()
        return 0

    lax.fori_loop(1, COLS, send_panel, 0)

    @pl.when(r != 0)
    def _():
        remote(xp_ref.at[c], yp_ref.at[me], ps, prs, 0, c).start()

    def bulk(lo, hi):
        def send(o, _):
            t = lax.rem(me + o, n)
            remote(x_ref.at[t], y_ref.at[me], xs, xr, t // COLS, t % COLS).start()
            return 0

        lax.fori_loop(lo, hi, send, 0)

    top.wait()

    @pl.when(r == 0)
    def _():
        yp_ref[pl.ds(me, 1)] = xp_ref[pl.ds(c, 1)]
        remote(yp_ref.at[pl.ds(0, n - 1)], yp_ref.at[pl.ds(0, n - 1)], ps, prs, 1, c).wait_recv()
        total = ft_ref[...]
        src = jnp.concatenate(
            [yp_ref[s * COLS : (s + 1) * COLS].reshape(COLS * CAPC, 2 * CAPP) for s in range(ROWS)],
            axis=1,
        )
        parts = parts3(src)
        for k in range(2):
            rpl = onehot(PW, idx_ref[2 + k : 3 + k, :])
            cpl = onehot(CB, idx_ref[4 + k : 5 + k, :CB])
            for part in parts:
                total = total + dot_nt(rpl, dot_nn(cpl, part).astype(BF16))
        xb_ref[...] = total

        @pl.when(c == 0)
        def _():
            pv_ref[0:16, :] = xb_ref[0:16, :]

            def piece(t, _):
                remote(
                    xb_ref.at[sixteenth(t)], pv_ref.at[sixteenth(t)], vs.at[0], vr.at[0],
                    t // 4, (t % 4) * 4,
                ).start()
                return 0

            lax.fori_loop(1, 16, piece, 0)

        def part_to(q, _):
            remote(
                xb_ref.at[quarter(q)], pr_ref.at[z, quarter(q)], qs, qr.at[z, q], y, q * 4 + z
            ).start()
            return 0

        @pl.when(y == 0)
        def _():
            pr_ref[pl.ds(z, 1), 0:64] = xb_ref[0:64, :].reshape(1, 64, CB)
            lax.fori_loop(1, 4, part_to, 0)

        @pl.when(y != 0)
        def _():
            lax.fori_loop(0, 4, part_to, 0)

        for o in range(1, 4):
            remote(xb_ref, xb_ref, bs.at[o - 1], br, o, c).start()

    mine = 4 * r + y

    @pl.when(z == 0)
    def _():
        @pl.when(mine != 0)
        def _():
            remote(pv_ref.at[sixteenth(mine)], pv_ref.at[sixteenth(mine)], vs.at[0], vr.at[0], r, c).wait_recv()

        for o in range(1, 4):
            remote(
                pv_ref.at[sixteenth(mine)], pv_ref.at[sixteenth(mine)], vt.at[o - 1], vr.at[0], r, y * 4 + o
            ).start()

    @pl.when(z != 0)
    def _():
        remote(pv_ref.at[sixteenth(mine)], pv_ref.at[sixteenth(mine)], vs.at[0], vr.at[0], r, c).wait_recv()

    def plane(o, _):
        t = lax.rem(mine + o, 16)
        remote(
            pv_ref.at[sixteenth(mine)], pv_ref.at[sixteenth(mine)], vs.at[1], vr.at[1],
            t // 4, (t % 4) * 4 + z,
        ).start()
        return 0

    lax.fori_loop(1, 16, plane, 0)

    @pl.when(jnp.logical_or(r != 0, me >= 4))
    def _():
        remote(pr_ref.at[z, quarter(y)], pr_ref.at[z, quarter(y)], qs, qr.at[z, y], r, c).wait_recv()

    def to_y(zz):
        for o in range(1, 4):
            remote(
                pr_ref.at[zz, quarter(y)], pr_ref.at[zz, quarter(y)], ds.at[2], qr.at[zz, y],
                r, lax.rem(y + o, 4) * 4 + z,
            ).start()

    for o in range(1, 4):
        remote(
            pr_ref.at[z, quarter(y)], pr_ref.at[z, quarter(y)], ds.at[1], qr.at[z, y],
            r, y * 4 + lax.rem(z + o, 4),
        ).start()
    to_y(z)
    bulk(1, n)
    for o in range(1, 4):
        zz = lax.rem(z + o, 4)
        remote(pr_ref.at[zz, quarter(y)], pr_ref.at[zz, quarter(y)], qs, qr.at[zz, y], r, c).wait_recv()
        to_y(zz)

    y_ref[pl.ds(me, 1)] = x_ref[pl.ds(me, 1)]

    remote(pv_ref.at[0:240], pv_ref.at[0:240], vs.at[1], vr.at[1], r, c).wait_recv()

    @pl.when(r != 0)
    def _():
        remote(xb_ref, xb_ref, bs.at[0], br, r, c).wait_recv()

    for zz in range(4):
        for o in range(1, 4):
            yy = lax.rem(y + o, 4)
            remote(pr_ref.at[zz, quarter(yy)], pr_ref.at[zz, quarter(yy)], qs, qr.at[zz, yy], r, c).wait_recv()
    remote(x_ref.at[pl.ds(0, n - 1)], y_ref.at[pl.ds(0, n - 1)], xs, xr, r, c).wait_recv()

    remote(x_ref.at[pl.ds(0, n - 1)], y_ref.at[pl.ds(0, n - 1)], xs, xr, r, c).wait_send()
    remote(pv_ref.at[0:240], pv_ref.at[0:240], vs.at[1], vr.at[1], r, c).wait_send()
    remote(pr_ref.at[0, 0:192], pr_ref.at[0, 0:192], ds.at[1], br, r, c).wait_send()
    remote(pr_ref.at[0:3], pr_ref.at[0:3], ds.at[2], br, r, c).wait_send()

    @pl.when(z == 0)
    def _():
        for o in range(1, 4):
            remote(pv_ref.at[0:16], pv_ref.at[0:16], vt.at[o - 1], br, r, c).wait_send()

    @pl.when(r != 0)
    def _():
        remote(xp_ref, yp_ref.at[pl.ds(0, COLS)], ps, prs, r, c).wait_send()

    @pl.when(r == 0)
    def _():
        remote(xp_ref.at[0:15], yp_ref.at[0:15], ps, prs, r, c).wait_send()

        @pl.when(y == 0)
        def _():
            remote(xb_ref.at[0:192], xb_ref.at[0:192], qs, br, r, c).wait_send()

        @pl.when(y != 0)
        def _():
            remote(xb_ref, xb_ref, qs, br, r, c).wait_send()

        @pl.when(c == 0)
        def _():
            remote(xb_ref.at[0:240], xb_ref.at[0:240], vs.at[0], br, r, c).wait_send()

        for o in range(1, 4):
            remote(xb_ref, xb_ref, bs.at[o - 1], br, r, c).wait_send()


def factorize(m_ref, pv):
    n = PW
    m_ref[:, :n] = pv
    m_ref[:, n:] = (iota((n, n), 0) == iota((n, n), 1)).astype(F32)
    for b0 in range(0, n, OB):
        lo = (b0 // 128) * 128
        hi = n + ((b0 + OB - 1) // 128) * 128 + 128
        R = [m_ref[b0 + 8 * i : b0 + 8 * i + 8, lo:hi] for i in range(OB // 8)]
        w = hi - lo
        sub = iota((8, 128), 0)
        sub1 = iota((8, 1), 0)
        for ib in range(OB // 8):
            b = b0 + 8 * ib
            at = b - lo
            C = [[jnp.broadcast_to(R[i][:, at + k : at + k + 1], (8, 128)) for i in range(ib, OB // 8)] for k in range(8)]
            for k in range(8):
                piv = jnp.broadcast_to(C[k][0][k : k + 1, :], (8, 128))
                rs = lax.rsqrt(piv)
                mul = [c * rs for c in C[k]]
                mul[0] = jnp.where(sub > k, mul[0], 0.0)
                for j in range(k + 1, 8):
                    t = jnp.broadcast_to(C[j][0][k : k + 1, :], (8, 128)) * rs
                    C[j] = [c - m * t for c, m in zip(C[j], mul)]
                rk = jnp.concatenate([jnp.broadcast_to(R[ib][k:k+1, q*128:(q+1)*128], (8,128)) * rs for q in range(w // 128)], axis=1)
                for i in range(ib, OB // 8):
                    m = jnp.concatenate([mul[i - ib]] * (w // 128), axis=1)
                    new = R[i] - m * rk
                    if i == ib:
                        new = jnp.where(jnp.concatenate([sub] * (w // 128), axis=1) == k, rk, new)
                    R[i] = new
        rows = jnp.concatenate(R, axis=0)
        below = (iota((OB, w), 1) + lo) < (b0 + iota((OB, w), 0))
        rows = jnp.where(below, 0.0, rows)
        m_ref[b0 : b0 + OB, lo:hi] = rows
        if lo:
            m_ref[b0 : b0 + OB, :lo] = jnp.zeros((OB, lo), F32)
        nb = b0 + OB
        if nb < n:
            l2 = (nb // 128) * 128
            upd = lax.dot_general(rows[:, l2 - lo : n - lo], rows[:, l2 - lo :], (((0,), (0,)), ((), ())), preferred_element_type=F32, precision=lax.Precision.HIGHEST)
            m_ref[nb:, l2:hi] = m_ref[nb:, l2:hi] - upd[nb - l2 :, :]


def final_kernel(pos, y_ref, idx_ref, f_ref, xb_ref, pr_ref, pv_ref, o_ref, m_ref):
    r = pos[0]
    c = pos[1]
    factorize(m_ref, pv_ref[...])
    inv = m_ref[:, PW:]

    @pl.when(c == 0)
    def _():
        for s in range(4):
            o_ref[s * 256 : (s + 1) * 256, :] = lax.dot_general(
                pr_ref[s], inv, (((0,), (1,)), ((), ())), preferred_element_type=F32,
                precision=lax.Precision.HIGHEST,
            )

        @pl.when(r == 0)
        def _():
            o_ref[:PW, :] = m_ref[:, :PW].T

    @pl.when(c != 0)
    def _():
        right = dot3(dot_nn, inv, xb_ref[...])
        ws = []
        for k in range(2):
            cpl = onehot(CB, idx_ref[4 + k : 5 + k, :CB])
            src = jnp.concatenate(
                [y_ref[s * COLS : (s + 1) * COLS, k].reshape(COLS * CAPC, CAPR) for s in range(ROWS)],
                axis=1,
            )
            ws.append([dot_nn(cpl, part).astype(BF16) for part in parts3(src)])
        for s in range(4):
            rows = slice(s * 256, (s + 1) * 256)
            left = dot3(dot_nn, inv, pr_ref[s])
            total = f_ref[rows, :] - dot3(dot_tn, left, right)
            for k in range(2):
                rpl = onehot(PW, idx_ref[k : k + 1, :] - s * 256)
                for w in ws[k]:
                    total = total + dot_nt(rpl, w)
            o_ref[rows, :] = total

        @pl.when(r == 0)
        def _():
            o_ref[:PW, :] = jnp.zeros((PW, CB), F32)


def vm():
    return pl.BlockSpec(memory_space=pltpu.VMEM)


def sm():
    return pl.BlockSpec(memory_space=pltpu.SMEM)


def shape(*s):
    return jax.ShapeDtypeStruct(s, F32)


def local_params():
    return pltpu.CompilerParams(vmem_limit_bytes=VMEM_LIMIT)


def remote_params(i):
    return pltpu.CompilerParams(
        vmem_limit_bytes=VMEM_LIMIT, collective_id=i, has_side_effects=True
    )


def pack(pos, u0, u1, maps):
    return pl.pallas_call(
        pack_kernel,
        out_shape=[
            shape(ROWS * COLS, 2, CAPC, CAPR),
            shape(COLS, CAPC, 2 * CAPP),
            jax.ShapeDtypeStruct((8, UR), jnp.int32),
        ],
        in_specs=[sm(), vm(), vm(), vm(), vm()],
        out_specs=[vm()] * 3,
        compiler_params=local_params(),
    )(pos, u0, u1, maps, maps.reshape(2 * COLS, UCB))


def move(x, xp, idx, f):
    dma = pltpu.SemaphoreType.DMA
    return pl.pallas_call(
        move_kernel,
        out_shape=[
            shape(ROWS * COLS, 2, CAPC, CAPR),
            shape(PW, CB),
            shape(4, PW, CB),
            shape(PW, CB),
        ],
        in_specs=[vm(), vm(), vm(), pl.BlockSpec(memory_space=pl.ANY)],
        out_specs=[vm()] * 4,
        scratch_shapes=[
            pltpu.VMEM((ROWS * COLS, CAPC, 2 * CAPP), F32),
            pltpu.VMEM((PW, CB), F32),
            dma, dma, dma, dma, dma((3,)), dma, dma, dma((4, 4)), dma((3,)), dma((2,)), dma((2,)),
            dma((3,)), dma,
        ],
        compiler_params=remote_params(1),
    )(x, xp, idx, f)


def final(pos, y, idx, f, xb, pr, pv):
    return pl.pallas_call(
        final_kernel,
        out_shape=shape(RB, CB),
        in_specs=[sm()] + [vm()] * 6,
        out_specs=vm(),
        scratch_shapes=[pltpu.VMEM((PW, 2 * PW), F32)],
        compiler_params=local_params(),
    )(pos, y, idx, f, xb, pr, pv)


def per_device(front_matrix, child_updates, child_map):
    pairs = [(s, s ^ 1) for s in range(4)]
    u1 = lax.ppermute(child_updates[0, 1], "front", pairs)
    m1 = lax.ppermute(child_map[0, 1], "front", pairs)
    maps = jnp.stack([child_map[0, 0], m1])
    pos = jnp.stack([lax.axis_index("row"), lax.axis_index("col")]).astype(jnp.int32)
    f = front_matrix[0]
    x, xp, idx = pack(pos, child_updates[0, 0], u1, maps)
    y, xb, pr, pv = move(x, xp, idx, f)
    return final(pos, y, idx, f, xb, pr, pv)[None]


def solution(mesh):
    in_specs = (P("front", "row", "col"), P("front", None, "row", "col"), P("front", None, None))
    return jax.shard_map(
        per_device, mesh=mesh, in_specs=in_specs, out_specs=P("front", "row", "col"), check_vma=False
    )
```

```python
import functools

import jax
import jax.numpy as jnp
from jax import lax
from jax.experimental import pallas as pl
from jax.experimental.pallas import tpu as pltpu
from jax.sharding import PartitionSpec as P

PW = 256
ROWS = 4
COLS = 16
RB = 1024
CB = 256
UR = 512
UCB = 128
CAPR = 128
CAPC = 16
CAPP = 64
OB = 64
MESH = pl.DeviceIdType.MESH
F32 = jnp.float32
BF16 = jnp.bfloat16
VMEM_LIMIT = 48 * 1024 * 1024


def parts3(x):
    hi = x.astype(BF16)
    rest = x - hi.astype(F32)
    mid = rest.astype(BF16)
    low = (rest - mid.astype(F32)).astype(BF16)
    return hi, mid, low


def dot_nt(a, b):
    return lax.dot_general(a, b, (((1,), (1,)), ((), ())), preferred_element_type=F32)


def dot_nn(a, b):
    return lax.dot_general(a, b, (((1,), (0,)), ((), ())), preferred_element_type=F32)


def dot_tn(a, b):
    return lax.dot_general(a, b, (((0,), (0,)), ((), ())), preferred_element_type=F32)


def split2(x):
    hi = x.astype(BF16)
    return hi, (x - hi.astype(F32)).astype(BF16)


def dot3(dot, a, b):
    ah, al = split2(a)
    bh, bl = split2(b)
    return dot(ah, bh) + (dot(ah, bl) + dot(al, bh))


def iota(shape, dim):
    return lax.broadcasted_iota(jnp.int32, shape, dim)


def onehot(rows, index):
    return (iota((rows, index.shape[1]), 0) == index).astype(F32).astype(BF16)


def before(n):
    return (iota((n, n), 0) < iota((n, n), 1)).astype(F32).astype(BF16)


def ranked_slot(dest, groups, cap):
    hit = iota((groups, dest.shape[1]), 0) == dest
    hits = hit.astype(F32)
    count = dot_nn(hits.astype(BF16), before(dest.shape[1]))
    rank = jnp.sum(jnp.where(hit, count, 0.0), axis=0, keepdims=True)
    return dest * cap + rank.astype(jnp.int32)


def factorize(m_ref, pv):
    n = PW
    m_ref[:, :n] = pv
    m_ref[:, n:] = (iota((n, n), 0) == iota((n, n), 1)).astype(F32)
    for b0 in range(0, n, OB):
        lo = (b0 // 128) * 128
        hi = n + ((b0 + OB - 1) // 128) * 128 + 128
        R = [m_ref[b0 + 8 * i : b0 + 8 * i + 8, lo:hi] for i in range(OB // 8)]
        w = hi - lo
        sub = iota((8, 128), 0)
        sub1 = iota((8, 1), 0)
        for ib in range(OB // 8):
            b = b0 + 8 * ib
            at = b - lo
            C = [[jnp.broadcast_to(R[i][:, at + k : at + k + 1], (8, 128)) for i in range(ib, OB // 8)] for k in range(8)]
            for k in range(8):
                piv = jnp.broadcast_to(C[k][0][k : k + 1, :], (8, 128))
                rs = lax.rsqrt(piv)
                mul = [c * rs for c in C[k]]
                mul[0] = jnp.where(sub > k, mul[0], 0.0)
                for j in range(k + 1, 8):
                    t = jnp.broadcast_to(C[j][0][k : k + 1, :], (8, 128)) * rs
                    C[j] = [c - m * t for c, m in zip(C[j], mul)]
                rk = jnp.concatenate([jnp.broadcast_to(R[ib][k:k+1, q*128:(q+1)*128], (8,128)) * rs for q in range(w // 128)], axis=1)
                for i in range(ib, OB // 8):
                    m = jnp.concatenate([mul[i - ib]] * (w // 128), axis=1)
                    new = R[i] - m * rk
                    if i == ib:
                        new = jnp.where(jnp.concatenate([sub] * (w // 128), axis=1) == k, rk, new)
                    R[i] = new
        rows = jnp.concatenate(R, axis=0)
        below = (iota((OB, w), 1) + lo) < (b0 + iota((OB, w), 0))
        rows = jnp.where(below, 0.0, rows)
        m_ref[b0 : b0 + OB, lo:hi] = rows
        if lo:
            m_ref[b0 : b0 + OB, :lo] = jnp.zeros((OB, lo), F32)
        nb = b0 + OB
        if nb < n:
            l2 = (nb // 128) * 128
            upd = lax.dot_general(rows[:, l2 - lo : n - lo], rows[:, l2 - lo :], (((0,), (0,)), ((), ())), preferred_element_type=F32, precision=lax.Precision.HIGHEST)
            m_ref[nb:, l2:hi] = m_ref[nb:, l2:hi] - upd[nb - l2 :, :]


def kernel(
    m_ref, u_ref, f_hbm, o_ref,
    u0_ref, u1_ref, mp_ref, f_ref, x_ref, y_ref, xp_ref, yp_ref, xb_ref, pr_ref, pv_ref, e_ref,
    lo_sem, us, ur, xs, xr, ps, prs, bs, br, qs, qr, ds, vs, vr, vt,
):
    f = lax.axis_index("front")
    r = lax.axis_index("row")
    c = lax.axis_index("col")
    y = c // 4
    z = c % 4
    me = r * COLS + c
    n = ROWS * COLS
    other = f + 1 - 2 * (f % 2)
    load_u = pltpu.make_async_copy(u_ref.at[0], u0_ref, lo_sem.at[0])
    load_u.start()
    load_f = pltpu.make_async_copy(f_hbm, f_ref, lo_sem.at[1])
    load_f.start()

    barrier = pltpu.get_barrier_semaphore()
    partner = {"front": other, "row": r, "col": c}
    pl.semaphore_signal(barrier, inc=1, device_id=partner, device_id_type=MESH)

    def greet(o, _):
        t = lax.rem(me + o, n)
        pl.semaphore_signal(
            barrier, inc=1, device_id={"row": t // COLS, "col": t % COLS}, device_id_type=MESH
        )
        return 0

    lax.fori_loop(1, n, greet, 0)
    pl.semaphore_wait(barrier, n)

    def remote(src, dst, s_sem, r_sem, row, col):
        return pltpu.make_async_remote_copy(
            src_ref=src, dst_ref=dst, send_sem=s_sem, recv_sem=r_sem,
            device_id={"row": row, "col": col}, device_id_type=MESH,
        )

    def quarter(i):
        return pl.ds(pl.multiple_of(i * 64, 64), 64)

    def sixteenth(i):
        return pl.ds(pl.multiple_of(i * 16, 16), 16)

    swap_m = pltpu.make_async_remote_copy(
        src_ref=m_ref, dst_ref=mp_ref, send_sem=us.at[0], recv_sem=ur.at[0],
        device_id=partner, device_id_type=MESH,
    )
    swap_m.start()
    swap_u = pltpu.make_async_remote_copy(
        src_ref=u_ref.at[1], dst_ref=u1_ref, send_sem=us.at[1], recv_sem=ur.at[1],
        device_id=partner, device_id_type=MESH,
    )
    swap_u.start()

    def maps(k):
        return m_ref if k == 0 else mp_ref

    panel = None
    columns = []
    for k in range(2):
        if k == 0:
            load_u.wait()
        else:
            swap_m.wait()
            swap_u.wait()
        mr = maps(k)[k : k + 1, pl.ds(pl.multiple_of(r * UR, UR), UR)]
        mc = maps(k)[k : k + 1, pl.ds(pl.multiple_of(c * UCB, UCB), UCB)]
        cp = onehot(COLS * CAPC, ranked_slot(mc // CB, COLS, CAPC))
        first = mr < PW
        place = ranked_slot(jnp.where(first, 0, 1), 8, 0) + CAPP * k
        pp = onehot(2 * CAPP, jnp.where(first, place, -1))
        values = u0_ref[...] if k == 0 else u1_ref[...]
        columns.append([dot_nt(cp, part).astype(BF16) for part in parts3(values)])
        for t in columns[k]:
            piece = dot_nt(t, pp)
            panel = piece if panel is None else panel + piece
    xp_ref[...] = panel.reshape(COLS, CAPC, 2 * CAPP)

    def send_panel(o, _):
        t = lax.rem(c + o, COLS)
        remote(xp_ref.at[t], yp_ref.at[me], ps, prs, 0, t).start()
        return 0

    lax.fori_loop(1, COLS, send_panel, 0)

    @pl.when(r != 0)
    def _():
        remote(xp_ref.at[c], yp_ref.at[me], ps, prs, 0, c).start()

    for k in range(2):
        mr = maps(k)[k : k + 1, pl.ds(pl.multiple_of(r * UR, UR), UR)]
        rp = onehot(UR, ranked_slot(mr // RB, 8, CAPR))
        x = None
        for t in columns[k]:
            piece = dot_nt(t, rp)
            x = piece if x is None else x + piece
        for dst in range(ROWS):
            x_ref[dst * COLS : (dst + 1) * COLS, k] = x[
                :, dst * CAPR : (dst + 1) * CAPR
            ].reshape(COLS, CAPC, CAPR)

    def send_bulk(o, _):
        t = lax.rem(me + o, n)
        remote(x_ref.at[t], y_ref.at[me], xs, xr, t // COLS, t % COLS).start()
        return 0

    lax.fori_loop(1, n, send_bulk, 0)
    y_ref[pl.ds(me, 1)] = x_ref[pl.ds(me, 1)]

    mi = jnp.concatenate(
        [maps(k)[k : k + 1, s * UR : (s + 1) * UR] for k in range(2) for s in range(ROWS)], axis=0
    )
    mj = jnp.concatenate(
        [maps(k)[k : k + 1, s * UCB : (s + 1) * UCB] for k in range(2) for s in range(COLS)], axis=0
    )
    child = iota((8, UR), 0) // ROWS

    def slots(hit, base):
        rank = dot_nn(hit.astype(F32).astype(BF16), before(hit.shape[1])).astype(jnp.int32)
        return jnp.where(hit, rank + base, -1)

    slot = slots((mi // RB) == r, 0)
    pslot = slots(mi < PW, CAPP * child)
    slot16 = slots((mj // CB) == c, CAPC * (iota((2 * COLS, UCB), 0) % COLS))
    eight = iota((8, 1), 0)
    row_of = []
    prow_of = []
    col_of = []
    for k in range(2):
        rows = []
        prows = []
        for s in range(ROWS):
            row = k * ROWS + s
            v = mi[row : row + 1, :]
            vals = jnp.where(eight == 0, (v % RB) // 256, v % 256).astype(F32).astype(BF16)
            got = dot_nt(vals, onehot(CAPR, slot[row : row + 1, :]))
            rows.append(got[0:1, :] * 256.0 + got[1:2, :])
            vals = jnp.broadcast_to((v % 256 + 1).astype(F32).astype(BF16), (8, UR))
            got = dot_nt(vals, onehot(2 * CAPP, pslot[row : row + 1, :]))
            prows.append(got[0:1, :] - 1.0)
        row_of.append(jnp.concatenate(rows, axis=1).astype(jnp.int32))
        prow_of.append(jnp.concatenate(prows, axis=1).astype(jnp.int32))
        tslot = jnp.concatenate(
            [slot16[k * COLS + s : k * COLS + s + 1, :] for s in range(COLS)], axis=1
        )
        v = (maps(k)[k : k + 1, :] % CB).astype(F32).astype(BF16)
        got = dot_nt(jnp.broadcast_to(v, (8, COLS * UCB)), onehot(COLS * CAPC, tslot))
        col_of.append(got[0:1, :].astype(jnp.int32))
    cpl = [onehot(CB, col_of[k]) for k in range(2)]

    load_f.wait()

    @pl.when(r == 0)
    def _():
        yp_ref[pl.ds(me, 1)] = xp_ref[pl.ds(c, 1)]
        remote(yp_ref.at[pl.ds(0, n - 1)], yp_ref.at[pl.ds(0, n - 1)], ps, prs, 1, c).wait_recv()
        total = f_ref[:PW, :]
        src = jnp.concatenate(
            [yp_ref[s * COLS : (s + 1) * COLS].reshape(COLS * CAPC, 2 * CAPP) for s in range(ROWS)],
            axis=1,
        )
        parts = parts3(src)
        for k in range(2):
            rpl = onehot(PW, prow_of[k])
            for part in parts:
                total = total + dot_nt(rpl, dot_nn(cpl[k], part).astype(BF16))
        xb_ref[...] = total

        @pl.when(c == 0)
        def _():
            pv_ref[0:16, :] = xb_ref[0:16, :]

            def piece(t, _):
                remote(
                    xb_ref.at[sixteenth(t)], pv_ref.at[sixteenth(t)], vs.at[0], vr.at[0],
                    t // 4, (t % 4) * 4,
                ).start()
                return 0

            lax.fori_loop(1, 16, piece, 0)

        def part_to(q, _):
            remote(
                xb_ref.at[quarter(q)], pr_ref.at[z, quarter(q)], qs, qr.at[z, q], y, q * 4 + z
            ).start()
            return 0

        @pl.when(y == 0)
        def _():
            pr_ref[pl.ds(z, 1), 0:64] = xb_ref[0:64, :].reshape(1, 64, CB)
            lax.fori_loop(1, 4, part_to, 0)

        @pl.when(y != 0)
        def _():
            lax.fori_loop(0, 4, part_to, 0)

        for o in range(1, 4):
            remote(xb_ref, xb_ref, bs.at[o - 1], br, o, c).start()

    mine = 4 * r + y

    @pl.when(z == 0)
    def _():
        @pl.when(mine != 0)
        def _():
            remote(pv_ref.at[sixteenth(mine)], pv_ref.at[sixteenth(mine)], vs.at[0], vr.at[0], r, c).wait_recv()

        for o in range(1, 4):
            remote(
                pv_ref.at[sixteenth(mine)], pv_ref.at[sixteenth(mine)], vt.at[o - 1], vr.at[0], r, y * 4 + o
            ).start()

    @pl.when(z != 0)
    def _():
        remote(pv_ref.at[sixteenth(mine)], pv_ref.at[sixteenth(mine)], vs.at[0], vr.at[0], r, c).wait_recv()

    def plane(o, _):
        t = lax.rem(mine + o, 16)
        remote(
            pv_ref.at[sixteenth(mine)], pv_ref.at[sixteenth(mine)], vs.at[1], vr.at[1],
            t // 4, (t % 4) * 4 + z,
        ).start()
        return 0

    lax.fori_loop(1, 16, plane, 0)

    @pl.when(jnp.logical_or(r != 0, me >= 4))
    def _():
        remote(pr_ref.at[z, quarter(y)], pr_ref.at[z, quarter(y)], qs, qr.at[z, y], r, c).wait_recv()

    def to_y(zz):
        for o in range(1, 4):
            remote(
                pr_ref.at[zz, quarter(y)], pr_ref.at[zz, quarter(y)], ds.at[2], qr.at[zz, y],
                r, lax.rem(y + o, 4) * 4 + z,
            ).start()

    for o in range(1, 4):
        remote(
            pr_ref.at[z, quarter(y)], pr_ref.at[z, quarter(y)], ds.at[1], qr.at[z, y],
            r, y * 4 + lax.rem(z + o, 4),
        ).start()
    to_y(z)
    for o in range(1, 4):
        zz = lax.rem(z + o, 4)
        remote(pr_ref.at[zz, quarter(y)], pr_ref.at[zz, quarter(y)], qs, qr.at[zz, y], r, c).wait_recv()
        to_y(zz)

    remote(pv_ref.at[0:240], pv_ref.at[0:240], vs.at[1], vr.at[1], r, c).wait_recv()
    factorize(e_ref, pv_ref[...])
    inv = e_ref[:, PW:]

    remote(x_ref.at[pl.ds(0, n - 1)], y_ref.at[pl.ds(0, n - 1)], xs, xr, r, c).wait_recv()

    @pl.when(c != 0)
    def _():
        placed = []
        for k in range(2):
            src = jnp.concatenate(
                [y_ref[s * COLS : (s + 1) * COLS, k].reshape(COLS * CAPC, CAPR) for s in range(ROWS)],
                axis=1,
            )
            placed.append([dot_nn(cpl[k], part).astype(BF16) for part in parts3(src)])
        for s in range(4):
            rows = slice(s * 256, (s + 1) * 256)
            total = f_ref[rows, :]
            for k in range(2):
                rpl = onehot(PW, row_of[k] - s * 256)
                for w in placed[k]:
                    total = total + dot_nt(rpl, w)
            f_ref[rows, :] = total

    @pl.when(r != 0)
    def _():
        remote(xb_ref, xb_ref, bs.at[0], br, r, c).wait_recv()

    for zz in range(4):
        for o in range(1, 4):
            yy = lax.rem(y + o, 4)
            remote(
                pr_ref.at[zz, quarter(yy)], pr_ref.at[zz, quarter(yy)], qs, qr.at[zz, yy], r, c
            ).wait_recv()

    @pl.when(c == 0)
    def _():
        for s in range(4):
            o_ref[s * 256 : (s + 1) * 256, :] = lax.dot_general(
                pr_ref[s], inv, (((0,), (1,)), ((), ())), preferred_element_type=F32,
                precision=lax.Precision.HIGHEST,
            )

        @pl.when(r == 0)
        def _():
            o_ref[:PW, :] = e_ref[:, :PW].T

    @pl.when(c != 0)
    def _():
        right = dot3(dot_nn, inv, xb_ref[...])
        for s in range(4):
            rows = slice(s * 256, (s + 1) * 256)
            left = dot3(dot_nn, inv, pr_ref[s])
            o_ref[rows, :] = f_ref[rows, :] - dot3(dot_tn, left, right)

        @pl.when(r == 0)
        def _():
            o_ref[:PW, :] = jnp.zeros((PW, CB), F32)

    remote(x_ref.at[pl.ds(0, n - 1)], y_ref.at[pl.ds(0, n - 1)], xs, xr, r, c).wait_send()
    remote(pv_ref.at[0:240], pv_ref.at[0:240], vs.at[1], vr.at[1], r, c).wait_send()
    remote(pr_ref.at[0, 0:192], pr_ref.at[0, 0:192], ds.at[1], br, r, c).wait_send()
    remote(pr_ref.at[0:3], pr_ref.at[0:3], ds.at[2], br, r, c).wait_send()

    @pl.when(z == 0)
    def _():
        for o in range(1, 4):
            remote(pv_ref.at[0:16], pv_ref.at[0:16], vt.at[o - 1], br, r, c).wait_send()

    @pl.when(r != 0)
    def _():
        remote(xp_ref, yp_ref.at[pl.ds(0, COLS)], ps, prs, r, c).wait_send()

    @pl.when(r == 0)
    def _():
        remote(xp_ref.at[0:15], yp_ref.at[0:15], ps, prs, r, c).wait_send()

        @pl.when(y == 0)
        def _():
            remote(xb_ref.at[0:192], xb_ref.at[0:192], qs, br, r, c).wait_send()

        @pl.when(y != 0)
        def _():
            remote(xb_ref, xb_ref, qs, br, r, c).wait_send()

        @pl.when(c == 0)
        def _():
            remote(xb_ref.at[0:240], xb_ref.at[0:240], vs.at[0], br, r, c).wait_send()

        for o in range(1, 4):
            remote(xb_ref, xb_ref, bs.at[o - 1], br, r, c).wait_send()


def shape(*s):
    return jax.ShapeDtypeStruct(s, F32)


def per_device(front_matrix, child_updates, child_map):
    dma = pltpu.SemaphoreType.DMA
    out = pl.pallas_call(
        kernel,
        out_shape=shape(RB, CB),
        in_specs=[
            pl.BlockSpec(memory_space=pltpu.VMEM),
            pl.BlockSpec(memory_space=pl.ANY),
            pl.BlockSpec(memory_space=pl.ANY),
        ],
        out_specs=pl.BlockSpec(memory_space=pltpu.VMEM),
        scratch_shapes=[
            pltpu.VMEM((UR, UCB), F32),
            pltpu.VMEM((UR, UCB), F32),
            pltpu.VMEM((2, ROWS * UR), jnp.int32),
            pltpu.VMEM((RB, CB), F32),
            pltpu.VMEM((ROWS * COLS, 2, CAPC, CAPR), F32),
            pltpu.VMEM((ROWS * COLS, 2, CAPC, CAPR), F32),
            pltpu.VMEM((COLS, CAPC, 2 * CAPP), F32),
            pltpu.VMEM((ROWS * COLS, CAPC, 2 * CAPP), F32),
            pltpu.VMEM((PW, CB), F32),
            pltpu.VMEM((4, PW, CB), F32),
            pltpu.VMEM((PW, CB), F32),
            pltpu.VMEM((PW, 2 * PW), F32),
            dma((2,)), dma((2,)), dma((2,)),
            dma, dma, dma, dma, dma((3,)), dma, dma, dma((4, 4)), dma((3,)), dma((2,)), dma((2,)),
            dma((3,)),
        ],
        compiler_params=pltpu.CompilerParams(
            vmem_limit_bytes=VMEM_LIMIT, collective_id=1, has_side_effects=True
        ),
    )(child_map[0], child_updates[0], front_matrix[0])
    return out[None]


def solution(mesh):
    in_specs = (P("front", "row", "col"), P("front", None, "row", "col"), P("front", None, None))
    return jax.shard_map(
        per_device, mesh=mesh, in_specs=in_specs, out_specs=P("front", "row", "col"), check_vma=False
    )
```

```python
import functools

import jax
import jax.numpy as jnp
from jax import lax
from jax.experimental import pallas as pl
from jax.experimental.pallas import tpu as pltpu
from jax.sharding import PartitionSpec as P

PW = 256
ROWS = 4
COLS = 16
RB = 1024
CB = 256
UR = 512
UCB = 128
CAPR = 128
CAPC = 16
CAPP = 64
OB = 64
MESH = pl.DeviceIdType.MESH
F32 = jnp.float32
BF16 = jnp.bfloat16
VMEM_LIMIT = 60 * 1024 * 1024


def parts3(x):
    hi = x.astype(BF16)
    rest = x - hi.astype(F32)
    mid = rest.astype(BF16)
    low = (rest - mid.astype(F32)).astype(BF16)
    return hi, mid, low


def dot_nt(a, b):
    return lax.dot_general(a, b, (((1,), (1,)), ((), ())), preferred_element_type=F32)


def dot_nn(a, b):
    return lax.dot_general(a, b, (((1,), (0,)), ((), ())), preferred_element_type=F32)


def dot_tn(a, b):
    return lax.dot_general(a, b, (((0,), (0,)), ((), ())), preferred_element_type=F32)


def split2(x):
    hi = x.astype(BF16)
    return hi, (x - hi.astype(F32)).astype(BF16)


def dot3(dot, a, b):
    ah, al = split2(a)
    bh, bl = split2(b)
    return dot(ah, bh) + (dot(ah, bl) + dot(al, bh))


def iota(shape, dim):
    return lax.broadcasted_iota(jnp.int32, shape, dim)


def onehot(rows, index):
    return (iota((rows, index.shape[1]), 0) == index).astype(F32).astype(BF16)


def before(n):
    return (iota((n, n), 0) < iota((n, n), 1)).astype(F32).astype(BF16)


def ranked_slot(dest, groups, cap):
    hit = iota((groups, dest.shape[1]), 0) == dest
    hits = hit.astype(F32)
    count = dot_nn(hits.astype(BF16), before(dest.shape[1]))
    rank = jnp.sum(jnp.where(hit, count, 0.0), axis=0, keepdims=True)
    return dest * cap + rank.astype(jnp.int32)


def set_up(m_ref, pv):
    n = PW
    m_ref[:, :n] = pv
    m_ref[:, n:] = (iota((n, n), 0) == iota((n, n), 1)).astype(F32)


def eliminate(m_ref, begin, end):
    n = PW
    for b0 in range(begin, end, OB):
        lo = (b0 // 128) * 128
        hi = n + ((b0 + OB - 1) // 128) * 128 + 128
        R = [m_ref[b0 + 8 * i : b0 + 8 * i + 8, lo:hi] for i in range(OB // 8)]
        w = hi - lo
        sub = iota((8, 128), 0)
        sub1 = iota((8, 1), 0)
        for ib in range(OB // 8):
            b = b0 + 8 * ib
            at = b - lo
            C = [[jnp.broadcast_to(R[i][:, at + k : at + k + 1], (8, 128)) for i in range(ib, OB // 8)] for k in range(8)]
            for k in range(8):
                piv = jnp.broadcast_to(C[k][0][k : k + 1, :], (8, 128))
                rs = lax.rsqrt(piv)
                mul = [c * rs for c in C[k]]
                mul[0] = jnp.where(sub > k, mul[0], 0.0)
                for j in range(k + 1, 8):
                    t = jnp.broadcast_to(C[j][0][k : k + 1, :], (8, 128)) * rs
                    C[j] = [c - m * t for c, m in zip(C[j], mul)]
                rk = jnp.concatenate([jnp.broadcast_to(R[ib][k:k+1, q*128:(q+1)*128], (8,128)) * rs for q in range(w // 128)], axis=1)
                for i in range(ib, OB // 8):
                    m = jnp.concatenate([mul[i - ib]] * (w // 128), axis=1)
                    new = R[i] - m * rk
                    if i == ib:
                        new = jnp.where(jnp.concatenate([sub] * (w // 128), axis=1) == k, rk, new)
                    R[i] = new
        rows = jnp.concatenate(R, axis=0)
        below = (iota((OB, w), 1) + lo) < (b0 + iota((OB, w), 0))
        rows = jnp.where(below, 0.0, rows)
        m_ref[b0 : b0 + OB, lo:hi] = rows
        if lo:
            m_ref[b0 : b0 + OB, :lo] = jnp.zeros((OB, lo), F32)
        nb = b0 + OB
        if nb < n:
            l2 = (nb // 128) * 128
            upd = lax.dot_general(rows[:, l2 - lo : n - lo], rows[:, l2 - lo :], (((0,), (0,)), ((), ())), preferred_element_type=F32, precision=lax.Precision.HIGHEST)
            m_ref[nb:, l2:hi] = m_ref[nb:, l2:hi] - upd[nb - l2 :, :]


def kernel(
    m_ref, u_ref, f_hbm, o_ref,
    u0_ref, u1_ref, mp_ref, f_ref, x_ref, y_ref, xp_ref, yp_ref, xb_ref, pr_ref, pv_ref, e_ref,
    lo_sem, us, ur, xs, xr, ps, prs, bs, br, qs, qr, ds, vs, vr, vt,
):
    f = lax.axis_index("front")
    r = lax.axis_index("row")
    c = lax.axis_index("col")
    y = c // 4
    z = c % 4
    me = r * COLS + c
    n = ROWS * COLS
    other = f + 1 - 2 * (f % 2)
    load_u = pltpu.make_async_copy(u_ref.at[0], u0_ref, lo_sem.at[0])
    load_u.start()
    load_f = pltpu.make_async_copy(f_hbm, f_ref, lo_sem.at[1])
    load_f.start()

    barrier = pltpu.get_barrier_semaphore()
    partner = {"front": other, "row": r, "col": c}
    pl.semaphore_signal(barrier, inc=1, device_id=partner, device_id_type=MESH)

    def greet(o, _):
        t = lax.rem(me + o, n)
        pl.semaphore_signal(
            barrier, inc=1, device_id={"row": t // COLS, "col": t % COLS}, device_id_type=MESH
        )
        return 0

    lax.fori_loop(1, n, greet, 0)
    load_u.wait()
    columns = []

    def pack_columns(m, values):
        mc = m[:, pl.ds(pl.multiple_of(c * UCB, UCB), UCB)]
        cp = onehot(COLS * CAPC, ranked_slot(mc // CB, COLS, CAPC))
        columns.append([dot_nt(cp, part).astype(BF16) for part in parts3(values)])

    def pack_panel(k, m, panel):
        mr = m[:, pl.ds(pl.multiple_of(r * UR, UR), UR)]
        first = mr < PW
        place = ranked_slot(jnp.where(first, 0, 1), 8, 0) + CAPP * k
        pp = onehot(2 * CAPP, jnp.where(first, place, -1))
        for t in columns[k]:
            piece = dot_nt(t, pp)
            panel = piece if panel is None else panel + piece
        return panel

    pack_columns(m_ref.at[0:1], u0_ref[...])
    panel = pack_panel(0, m_ref.at[0:1], None)
    pl.semaphore_wait(barrier, n)

    def remote(src, dst, s_sem, r_sem, row, col):
        return pltpu.make_async_remote_copy(
            src_ref=src, dst_ref=dst, send_sem=s_sem, recv_sem=r_sem,
            device_id={"row": row, "col": col}, device_id_type=MESH,
        )

    def quarter(i):
        return pl.ds(pl.multiple_of(i * 64, 64), 64)

    def half(i):
        return pl.ds(i * 128, 128)

    def sixteenth(i):
        return pl.ds(pl.multiple_of(i * 16, 16), 16)

    swap_m = pltpu.make_async_remote_copy(
        src_ref=m_ref, dst_ref=mp_ref, send_sem=us.at[0], recv_sem=ur.at[0],
        device_id=partner, device_id_type=MESH,
    )
    swap_m.start()
    swap_u = pltpu.make_async_remote_copy(
        src_ref=u_ref.at[1], dst_ref=u1_ref, send_sem=us.at[1], recv_sem=ur.at[1],
        device_id=partner, device_id_type=MESH,
    )
    swap_u.start()

    def maps(k):
        return m_ref if k == 0 else mp_ref

    swap_m.wait()
    swap_u.wait()
    pack_columns(mp_ref.at[1:2], u1_ref[...])
    panel = pack_panel(1, mp_ref.at[1:2], panel)
    xp_ref[...] = panel.reshape(COLS, CAPC, 2 * CAPP)

    def send_panel(o, _):
        t = lax.rem(c + o, COLS)
        remote(xp_ref.at[t], yp_ref.at[me], ps, prs, 0, t).start()
        return 0

    lax.fori_loop(1, COLS, send_panel, 0)

    @pl.when(r != 0)
    def _():
        remote(xp_ref.at[c], yp_ref.at[me], ps, prs, 0, c).start()

    for k in range(2):
        mr = maps(k)[k : k + 1, pl.ds(pl.multiple_of(r * UR, UR), UR)]
        rp = onehot(UR, ranked_slot(mr // RB, 8, CAPR))
        x = None
        for t in columns[k]:
            piece = dot_nt(t, rp)
            x = piece if x is None else x + piece
        for dst in range(ROWS):
            x_ref[dst * COLS : (dst + 1) * COLS, k] = x[
                :, dst * CAPR : (dst + 1) * CAPR
            ].reshape(COLS, CAPC, CAPR)

    def send_bulk(o, _):
        t = lax.rem(me + o, n)

        @pl.when(t % COLS != 0)
        def _():
            remote(x_ref.at[t], y_ref.at[me], xs, xr, t // COLS, t % COLS).start()

        return 0

    lax.fori_loop(1, 64, send_bulk, 0)
    y_ref[pl.ds(me, 1)] = x_ref[pl.ds(me, 1)]

    mi = jnp.concatenate(
        [maps(k)[k : k + 1, s * UR : (s + 1) * UR] for k in range(2) for s in range(ROWS)], axis=0
    )
    mj = jnp.concatenate(
        [maps(k)[k : k + 1, s * UCB : (s + 1) * UCB] for k in range(2) for s in range(COLS)], axis=0
    )
    child = iota((8, UR), 0) // ROWS

    def slots(hit, base):
        rank = dot_nn(hit.astype(F32).astype(BF16), before(hit.shape[1])).astype(jnp.int32)
        return jnp.where(hit, rank + base, -1)

    slot = slots((mi // RB) == r, 0)
    pslot = slots(mi < PW, CAPP * child)
    slot16 = slots((mj // CB) == c, CAPC * (iota((2 * COLS, UCB), 0) % COLS))
    eight = iota((8, 1), 0)
    row_of = []
    prow_of = []
    col_of = []
    for k in range(2):
        rows = []
        prows = []
        for s in range(ROWS):
            row = k * ROWS + s
            v = mi[row : row + 1, :]
            vals = jnp.where(eight == 0, (v % RB) // 256, v % 256).astype(F32).astype(BF16)
            got = dot_nt(vals, onehot(CAPR, slot[row : row + 1, :]))
            rows.append(got[0:1, :] * 256.0 + got[1:2, :])
            vals = jnp.broadcast_to((v % 256 + 1).astype(F32).astype(BF16), (8, UR))
            got = dot_nt(vals, onehot(2 * CAPP, pslot[row : row + 1, :]))
            prows.append(got[0:1, :] - 1.0)
        row_of.append(jnp.concatenate(rows, axis=1).astype(jnp.int32))
        prow_of.append(jnp.concatenate(prows, axis=1).astype(jnp.int32))
        tslot = jnp.concatenate(
            [slot16[k * COLS + s : k * COLS + s + 1, :] for s in range(COLS)], axis=1
        )
        v = (maps(k)[k : k + 1, :] % CB).astype(F32).astype(BF16)
        got = dot_nt(jnp.broadcast_to(v, (8, COLS * UCB)), onehot(COLS * CAPC, tslot))
        col_of.append(got[0:1, :].astype(jnp.int32))
    cpl = [onehot(CB, col_of[k]) for k in range(2)]

    load_f.wait()

    @pl.when(r == 0)
    def _():
        yp_ref[pl.ds(me, 1)] = xp_ref[pl.ds(c, 1)]
        remote(yp_ref.at[pl.ds(0, n - 1)], yp_ref.at[pl.ds(0, n - 1)], ps, prs, 1, c).wait_recv()
        total = f_ref[:PW, :]
        src = jnp.concatenate(
            [yp_ref[s * COLS : (s + 1) * COLS].reshape(COLS * CAPC, 2 * CAPP) for s in range(ROWS)],
            axis=1,
        )
        parts = parts3(src)
        for k in range(2):
            rpl = onehot(PW, prow_of[k])
            for part in parts:
                total = total + dot_nt(rpl, dot_nn(cpl[k], part).astype(BF16))
        xb_ref[...] = total

        @pl.when(c == 0)
        def _():
            pv_ref[0:16, :] = xb_ref[0:16, :]

            def piece(t, _):
                remote(
                    xb_ref.at[sixteenth(t)], pv_ref.at[sixteenth(t)], vs.at[0], vr.at[0],
                    t // 4, (t % 4) * 4,
                ).start()
                return 0

            lax.fori_loop(1, 16, piece, 0)

        def part_to(q, _):
            remote(
                xb_ref.at[quarter(q)], pr_ref.at[z, quarter(q)], qs, qr.at[z, q], y, q * 4 + z
            ).start()
            return 0

        @pl.when(y == 0)
        def _():
            pr_ref[pl.ds(z, 1), 0:64] = xb_ref[0:64, :].reshape(1, 64, CB)
            lax.fori_loop(1, 4, part_to, 0)

        @pl.when(y != 0)
        def _():
            lax.fori_loop(0, 4, part_to, 0)

        def half_to(i, h, row):
            remote(xb_ref.at[half(h)], xb_ref.at[half(h)], bs.at[i], br.at[h], row, c).start()

        half_to(0, 0, 1)
        half_to(1, 1, 3)
        half_to(2, 1, 1)
        half_to(3, 0, 3)

    mine = 4 * r + y

    @pl.when(z == 0)
    def _():
        @pl.when(mine != 0)
        def _():
            remote(pv_ref.at[sixteenth(mine)], pv_ref.at[sixteenth(mine)], vs.at[0], vr.at[0], r, c).wait_recv()

        for o in range(1, 4):
            remote(
                pv_ref.at[sixteenth(mine)], pv_ref.at[sixteenth(mine)], vt.at[o - 1], vr.at[0], r, y * 4 + o
            ).start()

    @pl.when(z != 0)
    def _():
        remote(pv_ref.at[sixteenth(mine)], pv_ref.at[sixteenth(mine)], vs.at[0], vr.at[0], r, c).wait_recv()

    def plane(o, _):
        t = lax.rem(mine + o, 16)
        remote(
            pv_ref.at[sixteenth(mine)], pv_ref.at[sixteenth(mine)], vs.at[1], vr.at[1],
            t // 4, (t % 4) * 4 + z,
        ).start()
        return 0

    lax.fori_loop(1, 16, plane, 0)

    @pl.when(jnp.logical_or(r != 0, me >= 4))
    def _():
        remote(pr_ref.at[z, quarter(y)], pr_ref.at[z, quarter(y)], qs, qr.at[z, y], r, c).wait_recv()

    def to_y(zz):
        for o in range(1, 4):
            remote(
                pr_ref.at[zz, quarter(y)], pr_ref.at[zz, quarter(y)], ds.at[2], qr.at[zz, y],
                r, lax.rem(y + o, 4) * 4 + z,
            ).start()

    for o in range(1, 4):
        remote(
            pr_ref.at[z, quarter(y)], pr_ref.at[z, quarter(y)], ds.at[1], qr.at[z, y],
            r, y * 4 + lax.rem(z + o, 4),
        ).start()
    to_y(z)
    for o in range(1, 4):
        zz = lax.rem(z + o, 4)
        remote(pr_ref.at[zz, quarter(y)], pr_ref.at[zz, quarter(y)], qs, qr.at[zz, y], r, c).wait_recv()
        to_y(zz)

    @pl.when(r == 1)
    def _():
        remote(xb_ref.at[half(0)], xb_ref.at[half(0)], bs.at[0], br.at[0], r, c).wait_recv()
        remote(xb_ref.at[half(0)], xb_ref.at[half(0)], bs.at[0], br.at[0], 2, c).start()

    @pl.when(r == 3)
    def _():
        remote(xb_ref.at[half(1)], xb_ref.at[half(1)], bs.at[0], br.at[1], r, c).wait_recv()
        remote(xb_ref.at[half(1)], xb_ref.at[half(1)], bs.at[0], br.at[1], 2, c).start()

    remote(pv_ref.at[0:240], pv_ref.at[0:240], vs.at[1], vr.at[1], r, c).wait_recv()
    set_up(e_ref, pv_ref[...])
    eliminate(e_ref, 0, PW)
    inv = e_ref[:, PW:]

    @pl.when(c != 0)
    def _():
        remote(x_ref.at[pl.ds(0, n - 1)], y_ref.at[pl.ds(0, n - 1)], xs, xr, r, c).wait_recv()
        placed = []
        for k in range(2):
            src = jnp.concatenate(
                [y_ref[s * COLS : (s + 1) * COLS, k].reshape(COLS * CAPC, CAPR) for s in range(ROWS)],
                axis=1,
            )
            placed.append([dot_nn(cpl[k], part).astype(BF16) for part in parts3(src)])
        for s in range(4):
            rows = slice(s * 256, (s + 1) * 256)
            total = f_ref[rows, :]
            for k in range(2):
                rpl = onehot(PW, row_of[k] - s * 256)
                for w in placed[k]:
                    total = total + dot_nt(rpl, w)
            f_ref[rows, :] = total

    @pl.when(jnp.logical_or(r == 2, r == 3))
    def _():
        remote(xb_ref.at[half(0)], xb_ref.at[half(0)], bs.at[0], br.at[0], r, c).wait_recv()

    @pl.when(jnp.logical_or(r == 1, r == 2))
    def _():
        remote(xb_ref.at[half(1)], xb_ref.at[half(1)], bs.at[0], br.at[1], r, c).wait_recv()

    for zz in range(4):
        for o in range(1, 4):
            yy = lax.rem(y + o, 4)
            remote(
                pr_ref.at[zz, quarter(yy)], pr_ref.at[zz, quarter(yy)], qs, qr.at[zz, yy], r, c
            ).wait_recv()

    @pl.when(c == 0)
    def _():
        for s in range(4):
            o_ref[s * 256 : (s + 1) * 256, :] = lax.dot_general(
                pr_ref[s], inv, (((0,), (1,)), ((), ())), preferred_element_type=F32,
                precision=lax.Precision.HIGHEST,
            )

        @pl.when(r == 0)
        def _():
            o_ref[:PW, :] = e_ref[:, :PW].T

    @pl.when(c != 0)
    def _():
        right = dot3(dot_nn, inv, xb_ref[...])
        for s in range(4):
            rows = slice(s * 256, (s + 1) * 256)
            left = dot3(dot_nn, inv, pr_ref[s])
            o_ref[rows, :] = f_ref[rows, :] - dot3(dot_tn, left, right)

    @pl.when(c == 0)
    def _():
        remote(x_ref.at[0:60], y_ref.at[0:60], xs, xr, r, c).wait_send()

    @pl.when(c != 0)
    def _():
        remote(x_ref.at[0:59], y_ref.at[0:59], xs, xr, r, c).wait_send()

    remote(pv_ref.at[0:240], pv_ref.at[0:240], vs.at[1], vr.at[1], r, c).wait_send()
    remote(pr_ref.at[0, 0:192], pr_ref.at[0, 0:192], ds.at[1], br.at[0], r, c).wait_send()
    remote(pr_ref.at[0:3], pr_ref.at[0:3], ds.at[2], br.at[0], r, c).wait_send()

    @pl.when(z == 0)
    def _():
        for o in range(1, 4):
            remote(pv_ref.at[0:16], pv_ref.at[0:16], vt.at[o - 1], br.at[0], r, c).wait_send()

    @pl.when(r != 0)
    def _():
        remote(xp_ref, yp_ref.at[pl.ds(0, COLS)], ps, prs, r, c).wait_send()

    @pl.when(r == 0)
    def _():
        remote(xp_ref.at[0:15], yp_ref.at[0:15], ps, prs, r, c).wait_send()

        @pl.when(y == 0)
        def _():
            remote(xb_ref.at[0:192], xb_ref.at[0:192], qs, br.at[0], r, c).wait_send()

        @pl.when(y != 0)
        def _():
            remote(xb_ref, xb_ref, qs, br.at[0], r, c).wait_send()

        @pl.when(c == 0)
        def _():
            remote(xb_ref.at[0:240], xb_ref.at[0:240], vs.at[0], br.at[0], r, c).wait_send()

        for i in range(4):
            remote(xb_ref.at[0:128], xb_ref.at[0:128], bs.at[i], br.at[0], r, c).wait_send()

    @pl.when(jnp.logical_or(r == 1, r == 3))
    def _():
        remote(xb_ref.at[0:128], xb_ref.at[0:128], bs.at[0], br.at[0], r, c).wait_send()


def shape(*s):
    return jax.ShapeDtypeStruct(s, F32)


def per_device(front_matrix, child_updates, child_map):
    dma = pltpu.SemaphoreType.DMA
    out = pl.pallas_call(
        kernel,
        out_shape=shape(RB, CB),
        in_specs=[
            pl.BlockSpec(memory_space=pltpu.VMEM),
            pl.BlockSpec(memory_space=pl.ANY),
            pl.BlockSpec(memory_space=pl.ANY),
        ],
        out_specs=pl.BlockSpec(memory_space=pltpu.VMEM),
        scratch_shapes=[
            pltpu.VMEM((UR, UCB), F32),
            pltpu.VMEM((UR, UCB), F32),
            pltpu.VMEM((2, ROWS * UR), jnp.int32),
            pltpu.VMEM((RB, CB), F32),
            pltpu.VMEM((ROWS * COLS, 2, CAPC, CAPR), F32),
            pltpu.VMEM((ROWS * COLS, 2, CAPC, CAPR), F32),
            pltpu.VMEM((COLS, CAPC, 2 * CAPP), F32),
            pltpu.VMEM((ROWS * COLS, CAPC, 2 * CAPP), F32),
            pltpu.VMEM((PW, CB), F32),
            pltpu.VMEM((4, PW, CB), F32),
            pltpu.VMEM((PW, CB), F32),
            pltpu.VMEM((PW, 2 * PW), F32),
            dma((2,)), dma((2,)), dma((2,)),
            dma, dma, dma, dma, dma((4,)), dma((2,)), dma, dma((4, 4)), dma((3,)), dma((2,)), dma((2,)),
            dma((3,)),
        ],
        compiler_params=pltpu.CompilerParams(
            vmem_limit_bytes=VMEM_LIMIT, collective_id=1, has_side_effects=True
        ),
    )(child_map[0], child_updates[0], front_matrix[0])
    zero = jnp.logical_and(lax.axis_index("row") == 0, lax.axis_index("col") > 0)
    kept = jnp.logical_or(iota((RB, CB), 0) >= PW, jnp.logical_not(zero))
    return jnp.where(kept, out, 0.0)[None]


def solution(mesh):
    in_specs = (P("front", "row", "col"), P("front", None, "row", "col"), P("front", None, None))
    return jax.shard_map(
        per_device, mesh=mesh, in_specs=in_specs, out_specs=P("front", "row", "col"), check_vma=False
    )
```

```python
import functools

import jax
import jax.numpy as jnp
from jax import lax
from jax.experimental import pallas as pl
from jax.experimental.pallas import tpu as pltpu
from jax.sharding import PartitionSpec as P

PW = 256
ROWS = 4
COLS = 16
RB = 1024
CB = 256
UR = 512
UCB = 128
CAPR = 128
CAPC = 16
CAPP = 64
OB = 64
MESH = pl.DeviceIdType.MESH
F32 = jnp.float32
BF16 = jnp.bfloat16
VMEM_LIMIT = 48 * 1024 * 1024


def parts3(x):
    hi = x.astype(BF16)
    rest = x - hi.astype(F32)
    mid = rest.astype(BF16)
    low = (rest - mid.astype(F32)).astype(BF16)
    return hi, mid, low


def dot_nt(a, b):
    return lax.dot_general(a, b, (((1,), (1,)), ((), ())), preferred_element_type=F32)


def dot_nn(a, b):
    return lax.dot_general(a, b, (((1,), (0,)), ((), ())), preferred_element_type=F32)


def dot_tn(a, b):
    return lax.dot_general(a, b, (((0,), (0,)), ((), ())), preferred_element_type=F32)


def split2(x):
    hi = x.astype(BF16)
    return hi, (x - hi.astype(F32)).astype(BF16)


def dot3(dot, a, b):
    ah, al = split2(a)
    bh, bl = split2(b)
    return dot(ah, bh) + (dot(ah, bl) + dot(al, bh))


def iota(shape, dim):
    return lax.broadcasted_iota(jnp.int32, shape, dim)


def onehot(rows, index):
    return (iota((rows, index.shape[1]), 0) == index).astype(F32).astype(BF16)


def before(n):
    return (iota((n, n), 0) < iota((n, n), 1)).astype(F32).astype(BF16)


def ranked_slot(dest, groups, cap):
    hit = iota((groups, dest.shape[1]), 0) == dest
    hits = hit.astype(F32)
    count = dot_nn(hits.astype(BF16), before(dest.shape[1]))
    rank = jnp.sum(jnp.where(hit, count, 0.0), axis=0, keepdims=True)
    return dest * cap + rank.astype(jnp.int32)


def set_up(m_ref, pv):
    n = PW
    m_ref[:, :n] = pv
    m_ref[:, n:] = (iota((n, n), 0) == iota((n, n), 1)).astype(F32)


def eliminate(m_ref, begin, end):
    n = PW
    for b0 in range(begin, end, OB):
        lo = (b0 // 128) * 128
        hi = n + ((b0 + OB - 1) // 128) * 128 + 128
        R = [m_ref[b0 + 8 * i : b0 + 8 * i + 8, lo:hi] for i in range(OB // 8)]
        w = hi - lo
        sub = iota((8, 128), 0)
        sub1 = iota((8, 1), 0)
        for ib in range(OB // 8):
            b = b0 + 8 * ib
            at = b - lo
            C = [[jnp.broadcast_to(R[i][:, at + k : at + k + 1], (8, 128)) for i in range(ib, OB // 8)] for k in range(8)]
            for k in range(8):
                piv = jnp.broadcast_to(C[k][0][k : k + 1, :], (8, 128))
                rs = lax.rsqrt(piv)
                mul = [c * rs for c in C[k]]
                mul[0] = jnp.where(sub > k, mul[0], 0.0)
                for j in range(k + 1, 8):
                    t = jnp.broadcast_to(C[j][0][k : k + 1, :], (8, 128)) * rs
                    C[j] = [c - m * t for c, m in zip(C[j], mul)]
                rk = jnp.concatenate([jnp.broadcast_to(R[ib][k:k+1, q*128:(q+1)*128], (8,128)) * rs for q in range(w // 128)], axis=1)
                for i in range(ib, OB // 8):
                    m = jnp.concatenate([mul[i - ib]] * (w // 128), axis=1)
                    new = R[i] - m * rk
                    if i == ib:
                        new = jnp.where(jnp.concatenate([sub] * (w // 128), axis=1) == k, rk, new)
                    R[i] = new
        rows = jnp.concatenate(R, axis=0)
        below = (iota((OB, w), 1) + lo) < (b0 + iota((OB, w), 0))
        rows = jnp.where(below, 0.0, rows)
        m_ref[b0 : b0 + OB, lo:hi] = rows
        if lo:
            m_ref[b0 : b0 + OB, :lo] = jnp.zeros((OB, lo), F32)
        nb = b0 + OB
        if nb < n:
            l2 = (nb // 128) * 128
            upd = lax.dot_general(rows[:, l2 - lo : n - lo], rows[:, l2 - lo :], (((0,), (0,)), ((), ())), preferred_element_type=F32, precision=lax.Precision.HIGHEST)
            m_ref[nb:, l2:hi] = m_ref[nb:, l2:hi] - upd[nb - l2 :, :]


def kernel(
    m_ref, u_ref, f_ref, o_ref,
    u1_ref, mp_ref, a_ref, x_ref, y_ref, xp_ref, yp_ref, xb_ref, pr_ref, pv_ref, e_ref,
    us, ur, xs, xr, ps, prs, bs, br, qs, qr, ds, vs, vr, vt,
):
    f = lax.axis_index("front")
    r = lax.axis_index("row")
    c = lax.axis_index("col")
    y = c // 4
    z = c % 4
    me = r * COLS + c
    n = ROWS * COLS
    other = f + 1 - 2 * (f % 2)
    barrier = pltpu.get_barrier_semaphore()
    partner = {"front": other, "row": r, "col": c}
    pl.semaphore_signal(barrier, inc=1, device_id=partner, device_id_type=MESH)

    def greet(o, _):
        t = lax.rem(me + o, n)
        pl.semaphore_signal(
            barrier, inc=1, device_id={"row": t // COLS, "col": t % COLS}, device_id_type=MESH
        )
        return 0

    lax.fori_loop(1, n, greet, 0)
    columns = []

    def pack_columns(m, values):
        mc = m[:, pl.ds(pl.multiple_of(c * UCB, UCB), UCB)]
        cp = onehot(COLS * CAPC, ranked_slot(mc // CB, COLS, CAPC))
        columns.append([dot_nt(cp, part).astype(BF16) for part in parts3(values)])

    def pack_panel(k, m, panel):
        mr = m[:, pl.ds(pl.multiple_of(r * UR, UR), UR)]
        first = mr < PW
        place = ranked_slot(jnp.where(first, 0, 1), 8, 0) + CAPP * k
        pp = onehot(2 * CAPP, jnp.where(first, place, -1))
        for t in columns[k]:
            piece = dot_nt(t, pp)
            panel = piece if panel is None else panel + piece
        return panel

    def pack_rows(k, m):
        mr = m[:, pl.ds(pl.multiple_of(r * UR, UR), UR)]
        rp = onehot(UR, ranked_slot(mr // RB, 8, CAPR))
        x = None
        for t in columns[k]:
            piece = dot_nt(t, rp)
            x = piece if x is None else x + piece
        for dst in range(ROWS):
            x_ref[dst * COLS : (dst + 1) * COLS, k] = x[
                :, dst * CAPR : (dst + 1) * CAPR
            ].reshape(COLS, CAPC, CAPR)

    pack_columns(m_ref.at[0:1], u_ref[0])
    panel = pack_panel(0, m_ref.at[0:1], None)
    pack_rows(0, m_ref.at[0:1])
    pl.semaphore_wait(barrier, n)

    def remote(src, dst, s_sem, r_sem, row, col):
        return pltpu.make_async_remote_copy(
            src_ref=src, dst_ref=dst, send_sem=s_sem, recv_sem=r_sem,
            device_id={"row": row, "col": col}, device_id_type=MESH,
        )

    def quarter(i):
        return pl.ds(pl.multiple_of(i * 64, 64), 64)

    def half(i):
        return pl.ds(i * 128, 128)

    def sixteenth(i):
        return pl.ds(pl.multiple_of(i * 16, 16), 16)

    swap_m = pltpu.make_async_remote_copy(
        src_ref=m_ref, dst_ref=mp_ref, send_sem=us.at[0], recv_sem=ur.at[0],
        device_id=partner, device_id_type=MESH,
    )
    swap_m.start()
    swap_u = pltpu.make_async_remote_copy(
        src_ref=u_ref.at[1], dst_ref=u1_ref, send_sem=us.at[1], recv_sem=ur.at[1],
        device_id=partner, device_id_type=MESH,
    )
    swap_u.start()

    def maps(k):
        return m_ref if k == 0 else mp_ref

    def send_child(k, o):
        t = lax.rem(me + o, n)

        @pl.when(t % COLS != 0)
        def _():
            remote(x_ref.at[t, k], y_ref.at[me, k], xs, xr, t // COLS, t % COLS).start()

        return 0

    lax.fori_loop(1, 25, lambda o, _: send_child(0, o), 0)

    swap_m.wait()
    swap_u.wait()
    pack_columns(mp_ref.at[1:2], u1_ref[...])
    panel = pack_panel(1, mp_ref.at[1:2], panel)
    xp_ref[...] = panel.reshape(COLS, CAPC, 2 * CAPP)

    def send_panel(o, _):
        t = lax.rem(c + o, COLS)
        remote(xp_ref.at[t], yp_ref.at[me], ps, prs, 0, t).start()
        return 0

    lax.fori_loop(1, COLS, send_panel, 0)

    @pl.when(r != 0)
    def _():
        remote(xp_ref.at[c], yp_ref.at[me], ps, prs, 0, c).start()

    pack_rows(1, mp_ref.at[1:2])

    def send_bulk(o, _):
        t = lax.rem(me + o, n)

        @pl.when(t % COLS != 0)
        def _():
            remote(x_ref.at[t], y_ref.at[me], xs, xr, t // COLS, t % COLS).start()

        return 0

    lax.fori_loop(25, n, send_bulk, 0)
    lax.fori_loop(1, 25, lambda o, _: send_child(1, o), 0)
    y_ref[pl.ds(me, 1)] = x_ref[pl.ds(me, 1)]

    mi = jnp.concatenate(
        [maps(k)[k : k + 1, s * UR : (s + 1) * UR] for k in range(2) for s in range(ROWS)], axis=0
    )
    mj = jnp.concatenate(
        [maps(k)[k : k + 1, s * UCB : (s + 1) * UCB] for k in range(2) for s in range(COLS)], axis=0
    )
    child = iota((8, UR), 0) // ROWS

    def slots(hit, base):
        rank = dot_nn(hit.astype(F32).astype(BF16), before(hit.shape[1])).astype(jnp.int32)
        return jnp.where(hit, rank + base, -1)

    slot = slots((mi // RB) == r, 0)
    pslot = slots(mi < PW, CAPP * child)
    slot16 = slots((mj // CB) == c, CAPC * (iota((2 * COLS, UCB), 0) % COLS))
    eight = iota((8, 1), 0)
    row_of = []
    prow_of = []
    col_of = []
    for k in range(2):
        rows = []
        prows = []
        for s in range(ROWS):
            row = k * ROWS + s
            v = mi[row : row + 1, :]
            vals = jnp.where(eight == 0, (v % RB) // 256, v % 256).astype(F32).astype(BF16)
            got = dot_nt(vals, onehot(CAPR, slot[row : row + 1, :]))
            rows.append(got[0:1, :] * 256.0 + got[1:2, :])
            vals = jnp.broadcast_to((v % 256 + 1).astype(F32).astype(BF16), (8, UR))
            got = dot_nt(vals, onehot(2 * CAPP, pslot[row : row + 1, :]))
            prows.append(got[0:1, :] - 1.0)
        row_of.append(jnp.concatenate(rows, axis=1).astype(jnp.int32))
        prow_of.append(jnp.concatenate(prows, axis=1).astype(jnp.int32))
        tslot = jnp.concatenate(
            [slot16[k * COLS + s : k * COLS + s + 1, :] for s in range(COLS)], axis=1
        )
        v = (maps(k)[k : k + 1, :] % CB).astype(F32).astype(BF16)
        got = dot_nt(jnp.broadcast_to(v, (8, COLS * UCB)), onehot(COLS * CAPC, tslot))
        col_of.append(got[0:1, :].astype(jnp.int32))
    cpl = [onehot(CB, col_of[k]) for k in range(2)]

    @pl.when(r == 0)
    def _():
        yp_ref[pl.ds(me, 1)] = xp_ref[pl.ds(c, 1)]
        remote(yp_ref.at[pl.ds(0, n - 1)], yp_ref.at[pl.ds(0, n - 1)], ps, prs, 1, c).wait_recv()
        total = f_ref[:PW, :]
        src = jnp.concatenate(
            [yp_ref[s * COLS : (s + 1) * COLS].reshape(COLS * CAPC, 2 * CAPP) for s in range(ROWS)],
            axis=1,
        )
        parts = parts3(src)
        for k in range(2):
            rpl = onehot(PW, prow_of[k])
            for part in parts:
                total = total + dot_nt(rpl, dot_nn(cpl[k], part).astype(BF16))
        xb_ref[...] = total

        @pl.when(c == 0)
        def _():
            pv_ref[0:16, :] = xb_ref[0:16, :]

            def piece(t, _):
                remote(
                    xb_ref.at[sixteenth(t)], pv_ref.at[sixteenth(t)], vs.at[0], vr.at[0],
                    t // 4, (t % 4) * 4,
                ).start()
                return 0

            lax.fori_loop(1, 16, piece, 0)

        def part_to(q, _):
            remote(
                xb_ref.at[quarter(q)], pr_ref.at[z, quarter(q)], qs, qr.at[z, q], y, q * 4 + z
            ).start()
            return 0

        @pl.when(y == 0)
        def _():
            pr_ref[pl.ds(z, 1), 0:64] = xb_ref[0:64, :].reshape(1, 64, CB)
            lax.fori_loop(1, 4, part_to, 0)

        @pl.when(y != 0)
        def _():
            lax.fori_loop(0, 4, part_to, 0)

        def half_to(i, h, row):
            remote(xb_ref.at[half(h)], xb_ref.at[half(h)], bs.at[i], br.at[h], row, c).start()

        half_to(0, 0, 1)
        half_to(1, 1, 3)
        half_to(2, 1, 1)
        half_to(3, 0, 3)

    mine = 4 * r + y

    @pl.when(z == 0)
    def _():
        @pl.when(mine != 0)
        def _():
            remote(pv_ref.at[sixteenth(mine)], pv_ref.at[sixteenth(mine)], vs.at[0], vr.at[0], r, c).wait_recv()

        for o in range(1, 4):
            remote(
                pv_ref.at[sixteenth(mine)], pv_ref.at[sixteenth(mine)], vt.at[o - 1], vr.at[0], r, y * 4 + o
            ).start()

    @pl.when(z != 0)
    def _():
        remote(pv_ref.at[sixteenth(mine)], pv_ref.at[sixteenth(mine)], vs.at[0], vr.at[0], r, c).wait_recv()

    def plane(o, _):
        t = lax.rem(mine + o, 16)
        remote(
            pv_ref.at[sixteenth(mine)], pv_ref.at[sixteenth(mine)], vs.at[1], vr.at[1],
            t // 4, (t % 4) * 4 + z,
        ).start()
        return 0

    lax.fori_loop(1, 16, plane, 0)

    @pl.when(jnp.logical_or(r != 0, me >= 4))
    def _():
        remote(pr_ref.at[z, quarter(y)], pr_ref.at[z, quarter(y)], qs, qr.at[z, y], r, c).wait_recv()

    def to_y(zz):
        for o in range(1, 4):
            remote(
                pr_ref.at[zz, quarter(y)], pr_ref.at[zz, quarter(y)], ds.at[2], qr.at[zz, y],
                r, lax.rem(y + o, 4) * 4 + z,
            ).start()

    for o in range(1, 4):
        remote(
            pr_ref.at[z, quarter(y)], pr_ref.at[z, quarter(y)], ds.at[1], qr.at[z, y],
            r, y * 4 + lax.rem(z + o, 4),
        ).start()
    to_y(z)
    for o in range(1, 4):
        zz = lax.rem(z + o, 4)
        remote(pr_ref.at[zz, quarter(y)], pr_ref.at[zz, quarter(y)], qs, qr.at[zz, y], r, c).wait_recv()
        to_y(zz)

    @pl.when(r == 1)
    def _():
        remote(xb_ref.at[half(0)], xb_ref.at[half(0)], bs.at[0], br.at[0], r, c).wait_recv()
        remote(xb_ref.at[half(0)], xb_ref.at[half(0)], bs.at[0], br.at[0], 2, c).start()

    @pl.when(r == 3)
    def _():
        remote(xb_ref.at[half(1)], xb_ref.at[half(1)], bs.at[0], br.at[1], r, c).wait_recv()
        remote(xb_ref.at[half(1)], xb_ref.at[half(1)], bs.at[0], br.at[1], 2, c).start()

    remote(pv_ref.at[0:240], pv_ref.at[0:240], vs.at[1], vr.at[1], r, c).wait_recv()
    set_up(e_ref, pv_ref[...])
    eliminate(e_ref, 0, PW)
    inv = e_ref[:, PW:]

    @pl.when(c != 0)
    def _():
        remote(x_ref.at[pl.ds(0, n - 1)], y_ref.at[pl.ds(0, n - 1)], xs, xr, r, c).wait_recv()
        placed = []
        for k in range(2):
            src = jnp.concatenate(
                [y_ref[s * COLS : (s + 1) * COLS, k].reshape(COLS * CAPC, CAPR) for s in range(ROWS)],
                axis=1,
            )
            placed.append([dot_nn(cpl[k], part).astype(BF16) for part in split2(src)])
        for s in range(4):
            rows = slice(s * 256, (s + 1) * 256)
            total = f_ref[rows, :]
            for k in range(2):
                rpl = onehot(PW, row_of[k] - s * 256)
                for w in placed[k]:
                    total = total + dot_nt(rpl, w)
            a_ref[rows, :] = total

    @pl.when(jnp.logical_or(r == 2, r == 3))
    def _():
        remote(xb_ref.at[half(0)], xb_ref.at[half(0)], bs.at[0], br.at[0], r, c).wait_recv()

    @pl.when(jnp.logical_or(r == 1, r == 2))
    def _():
        remote(xb_ref.at[half(1)], xb_ref.at[half(1)], bs.at[0], br.at[1], r, c).wait_recv()

    for zz in range(4):
        for o in range(1, 4):
            yy = lax.rem(y + o, 4)
            remote(
                pr_ref.at[zz, quarter(yy)], pr_ref.at[zz, quarter(yy)], qs, qr.at[zz, yy], r, c
            ).wait_recv()

    @pl.when(c == 0)
    def _():
        for s in range(4):
            o_ref[s * 256 : (s + 1) * 256, :] = lax.dot_general(
                pr_ref[s], inv, (((0,), (1,)), ((), ())), preferred_element_type=F32,
                precision=lax.Precision.HIGHEST,
            )

        @pl.when(r == 0)
        def _():
            o_ref[:PW, :] = e_ref[:, :PW].T

    @pl.when(c != 0)
    def _():
        right = dot3(dot_nn, inv, xb_ref[...])
        for s in range(4):
            rows = slice(s * 256, (s + 1) * 256)
            left = dot3(dot_nn, inv, pr_ref[s])
            o_ref[rows, :] = a_ref[rows, :] - dot3(dot_tn, left, right)

    @pl.when(c == 0)
    def _():
        remote(x_ref.at[0:60], y_ref.at[0:60], xs, xr, r, c).wait_send()

    @pl.when(c != 0)
    def _():
        remote(x_ref.at[0:59], y_ref.at[0:59], xs, xr, r, c).wait_send()

    remote(pv_ref.at[0:240], pv_ref.at[0:240], vs.at[1], vr.at[1], r, c).wait_send()
    remote(pr_ref.at[0, 0:192], pr_ref.at[0, 0:192], ds.at[1], br.at[0], r, c).wait_send()
    remote(pr_ref.at[0:3], pr_ref.at[0:3], ds.at[2], br.at[0], r, c).wait_send()

    @pl.when(z == 0)
    def _():
        for o in range(1, 4):
            remote(pv_ref.at[0:16], pv_ref.at[0:16], vt.at[o - 1], br.at[0], r, c).wait_send()

    @pl.when(r != 0)
    def _():
        remote(xp_ref, yp_ref.at[pl.ds(0, COLS)], ps, prs, r, c).wait_send()

    @pl.when(r == 0)
    def _():
        remote(xp_ref.at[0:15], yp_ref.at[0:15], ps, prs, r, c).wait_send()

        @pl.when(y == 0)
        def _():
            remote(xb_ref.at[0:192], xb_ref.at[0:192], qs, br.at[0], r, c).wait_send()

        @pl.when(y != 0)
        def _():
            remote(xb_ref, xb_ref, qs, br.at[0], r, c).wait_send()

        @pl.when(c == 0)
        def _():
            remote(xb_ref.at[0:240], xb_ref.at[0:240], vs.at[0], br.at[0], r, c).wait_send()

        for i in range(4):
            remote(xb_ref.at[0:128], xb_ref.at[0:128], bs.at[i], br.at[0], r, c).wait_send()

    @pl.when(jnp.logical_or(r == 1, r == 3))
    def _():
        remote(xb_ref.at[0:128], xb_ref.at[0:128], bs.at[0], br.at[0], r, c).wait_send()


def shape(*s):
    return jax.ShapeDtypeStruct(s, F32)


def per_device(front_matrix, child_updates, child_map):
    dma = pltpu.SemaphoreType.DMA
    out = pl.pallas_call(
        kernel,
        out_shape=shape(RB, CB),
        in_specs=[
            pl.BlockSpec(memory_space=pltpu.VMEM),
            pl.BlockSpec(memory_space=pltpu.VMEM),
            pl.BlockSpec(memory_space=pltpu.VMEM),
        ],
        out_specs=pl.BlockSpec(memory_space=pltpu.VMEM),
        scratch_shapes=[
            pltpu.VMEM((UR, UCB), F32),
            pltpu.VMEM((2, ROWS * UR), jnp.int32),
            pltpu.VMEM((RB, CB), F32),
            pltpu.VMEM((ROWS * COLS, 2, CAPC, CAPR), F32),
            pltpu.VMEM((ROWS * COLS, 2, CAPC, CAPR), F32),
            pltpu.VMEM((COLS, CAPC, 2 * CAPP), F32),
            pltpu.VMEM((ROWS * COLS, CAPC, 2 * CAPP), F32),
            pltpu.VMEM((PW, CB), F32),
            pltpu.VMEM((4, PW, CB), F32),
            pltpu.VMEM((PW, CB), F32),
            pltpu.VMEM((PW, 2 * PW), F32),
            dma((2,)), dma((2,)),
            dma, dma, dma, dma, dma((4,)), dma((2,)), dma, dma((4, 4)), dma((3,)), dma((2,)), dma((2,)),
            dma((3,)),
        ],
        compiler_params=pltpu.CompilerParams(
            vmem_limit_bytes=VMEM_LIMIT, collective_id=1, has_side_effects=True
        ),
    )(child_map[0], child_updates[0], front_matrix[0])
    zero = jnp.logical_and(lax.axis_index("row") == 0, lax.axis_index("col") > 0)
    kept = jnp.logical_or(iota((RB, CB), 0) >= PW, jnp.logical_not(zero))
    return jnp.where(kept, out, 0.0)[None]


def solution(mesh):
    in_specs = (P("front", "row", "col"), P("front", None, "row", "col"), P("front", None, None))
    return jax.shard_map(
        per_device, mesh=mesh, in_specs=in_specs, out_specs=P("front", "row", "col"), check_vma=False
    )
```

```python
import functools

import jax
import jax.numpy as jnp
from jax import lax
from jax.experimental import pallas as pl
from jax.experimental.pallas import tpu as pltpu
from jax.sharding import PartitionSpec as P

PW = 256
ROWS = 4
COLS = 16
RB = 1024
CB = 256
UR = 512
UCB = 128
CAPR = 128
CAPC = 16
CAPP = 64
OB = 64
MESH = pl.DeviceIdType.MESH
F32 = jnp.float32
BF16 = jnp.bfloat16
VMEM_LIMIT = 48 * 1024 * 1024


def parts3(x):
    hi = x.astype(BF16)
    rest = x - hi.astype(F32)
    mid = rest.astype(BF16)
    low = (rest - mid.astype(F32)).astype(BF16)
    return hi, mid, low


def dot_nt(a, b):
    return lax.dot_general(a, b, (((1,), (1,)), ((), ())), preferred_element_type=F32)


def dot_nn(a, b):
    return lax.dot_general(a, b, (((1,), (0,)), ((), ())), preferred_element_type=F32)


def dot_tn(a, b):
    return lax.dot_general(a, b, (((0,), (0,)), ((), ())), preferred_element_type=F32)


def split2(x):
    hi = x.astype(BF16)
    return hi, (x - hi.astype(F32)).astype(BF16)


def dot3(dot, a, b):
    ah, al = split2(a)
    bh, bl = split2(b)
    return dot(ah, bh) + (dot(ah, bl) + dot(al, bh))


def iota(shape, dim):
    return lax.broadcasted_iota(jnp.int32, shape, dim)


def onehot(rows, index):
    return (iota((rows, index.shape[1]), 0) == index).astype(F32).astype(BF16)


def before(n):
    return (iota((n, n), 0) < iota((n, n), 1)).astype(F32).astype(BF16)


def ranked_slot(dest, groups, cap):
    hit = iota((groups, dest.shape[1]), 0) == dest
    hits = hit.astype(F32)
    count = dot_nn(hits.astype(BF16), before(dest.shape[1]))
    rank = jnp.sum(jnp.where(hit, count, 0.0), axis=0, keepdims=True)
    return dest * cap + rank.astype(jnp.int32)


def set_up(m_ref, pv):
    n = PW
    m_ref[:, :n] = pv


def eliminate(m_ref, begin, end):
    n = PW
    for b0 in range(begin, end, OB):
        lo = (b0 // 128) * 128
        hi = n + ((b0 + OB - 1) // 128) * 128 + 128
        R = [m_ref[b0 + 8 * i : b0 + 8 * i + 8, lo:hi] for i in range(OB // 8)]
        w = hi - lo
        sub = iota((8, 128), 0)
        sub1 = iota((8, 1), 0)
        for ib in range(OB // 8):
            b = b0 + 8 * ib
            at = b - lo
            C = [[jnp.broadcast_to(R[i][:, at + k : at + k + 1], (8, 128)) for i in range(ib, OB // 8)] for k in range(8)]
            for k in range(8):
                piv = jnp.broadcast_to(C[k][0][k : k + 1, :], (8, 128))
                rs = lax.rsqrt(piv)
                mul = [c * rs for c in C[k]]
                mul[0] = jnp.where(sub > k, mul[0], 0.0)
                for j in range(k + 1, 8):
                    t = jnp.broadcast_to(C[j][0][k : k + 1, :], (8, 128)) * rs
                    C[j] = [c - m * t for c, m in zip(C[j], mul)]
                rk = jnp.concatenate([jnp.broadcast_to(R[ib][k:k+1, q*128:(q+1)*128], (8,128)) * rs for q in range(w // 128)], axis=1)
                for i in range(ib, OB // 8):
                    m = jnp.concatenate([mul[i - ib]] * (w // 128), axis=1)
                    new = R[i] - m * rk
                    if i == ib:
                        new = jnp.where(jnp.concatenate([sub] * (w // 128), axis=1) == k, rk, new)
                    R[i] = new
        rows = jnp.concatenate(R, axis=0)
        below = (iota((OB, w), 1) + lo) < (b0 + iota((OB, w), 0))
        rows = jnp.where(below, 0.0, rows)
        m_ref[b0 : b0 + OB, lo:hi] = rows
        if lo:
            m_ref[b0 : b0 + OB, :lo] = jnp.zeros((OB, lo), F32)
        nb = b0 + OB
        if nb < n:
            l2 = (nb // 128) * 128
            upd = lax.dot_general(rows[:, l2 - lo : n - lo], rows[:, l2 - lo :], (((0,), (0,)), ((), ())), preferred_element_type=F32, precision=lax.Precision.HIGHEST)
            m_ref[nb:, l2:hi] = m_ref[nb:, l2:hi] - upd[nb - l2 :, :]


def kernel(
    m_ref, u_ref, f_ref, o_ref,
    u1_ref, mp_ref, place_ref, a_ref, x_ref, y_ref, xp_ref, yp_ref, xb_ref, pr_ref, pv_ref, e_ref,
    us, ur, xs, xr, ps, prs, bs, br, qs, qr, ds, vs, vr, vt,
):
    f = lax.axis_index("front")
    r = lax.axis_index("row")
    c = lax.axis_index("col")
    y = c // 4
    z = c % 4
    me = r * COLS + c
    n = ROWS * COLS
    other = f + 1 - 2 * (f % 2)
    barrier = pltpu.get_barrier_semaphore()
    partner = {"front": other, "row": r, "col": c}
    pl.semaphore_signal(barrier, inc=1, device_id=partner, device_id_type=MESH)

    def greet(o, _):
        t = lax.rem(me + o, n)
        pl.semaphore_signal(
            barrier, inc=1, device_id={"row": t // COLS, "col": t % COLS}, device_id_type=MESH
        )
        return 0

    lax.fori_loop(1, n, greet, 0)
    columns = []

    def pack_columns(m, values):
        mc = m[:, pl.ds(pl.multiple_of(c * UCB, UCB), UCB)]
        cp = onehot(COLS * CAPC, ranked_slot(mc // CB, COLS, CAPC))
        columns.append([dot_nt(cp, part).astype(BF16) for part in parts3(values)])

    def pack_panel(k, m, panel):
        mr = m[:, pl.ds(pl.multiple_of(r * UR, UR), UR)]
        first = mr < PW
        place = ranked_slot(jnp.where(first, 0, 1), 8, 0) + CAPP * k
        pp = onehot(2 * CAPP, jnp.where(first, place, -1))
        for t in columns[k]:
            piece = dot_nt(t, pp)
            panel = piece if panel is None else panel + piece
        return panel

    def pack_rows(k, m):
        mr = m[:, pl.ds(pl.multiple_of(r * UR, UR), UR)]
        rp = onehot(UR, ranked_slot(mr // RB, 8, CAPR))
        x = None
        for t in columns[k]:
            piece = dot_nt(t, rp)
            x = piece if x is None else x + piece
        for dst in range(ROWS):
            x_ref[dst * COLS : (dst + 1) * COLS, k] = x[
                :, dst * CAPR : (dst + 1) * CAPR
            ].reshape(COLS, CAPC, CAPR)

    pack_columns(m_ref.at[0:1], u_ref[0])
    panel = pack_panel(0, m_ref.at[0:1], None)
    pack_rows(0, m_ref.at[0:1])
    pl.semaphore_wait(barrier, n)

    def remote(src, dst, s_sem, r_sem, row, col):
        return pltpu.make_async_remote_copy(
            src_ref=src, dst_ref=dst, send_sem=s_sem, recv_sem=r_sem,
            device_id={"row": row, "col": col}, device_id_type=MESH,
        )

    def quarter(i):
        return pl.ds(pl.multiple_of(i * 64, 64), 64)

    def half(i):
        return pl.ds(i * 128, 128)

    def sixteenth(i):
        return pl.ds(pl.multiple_of(i * 16, 16), 16)

    swap_m = pltpu.make_async_remote_copy(
        src_ref=m_ref, dst_ref=mp_ref, send_sem=us.at[0], recv_sem=ur.at[0],
        device_id=partner, device_id_type=MESH,
    )
    swap_m.start()
    swap_u = pltpu.make_async_remote_copy(
        src_ref=u_ref.at[1], dst_ref=u1_ref, send_sem=us.at[1], recv_sem=ur.at[1],
        device_id=partner, device_id_type=MESH,
    )
    swap_u.start()

    def maps(k):
        return m_ref if k == 0 else mp_ref

    def send_child(k, o):
        t = lax.rem(me + o, n)

        @pl.when(t % COLS != 0)
        def _():
            remote(x_ref.at[t, k], y_ref.at[me, k], xs, xr, t // COLS, t % COLS).start()

        return 0

    lax.fori_loop(1, 25, lambda o, _: send_child(0, o), 0)

    swap_m.wait()
    swap_u.wait()
    pack_columns(mp_ref.at[1:2], u1_ref[...])
    panel = pack_panel(1, mp_ref.at[1:2], panel)
    xp_ref[...] = panel.reshape(COLS, CAPC, 2 * CAPP)

    def send_panel(o, _):
        t = lax.rem(c + o, COLS)
        remote(xp_ref.at[t], yp_ref.at[me], ps, prs, 0, t).start()
        return 0

    lax.fori_loop(1, COLS, send_panel, 0)

    @pl.when(r != 0)
    def _():
        remote(xp_ref.at[c], yp_ref.at[me], ps, prs, 0, c).start()

    pack_rows(1, mp_ref.at[1:2])

    def send_bulk(o, _):
        t = lax.rem(me + o, n)

        @pl.when(t % COLS != 0)
        def _():
            remote(x_ref.at[t], y_ref.at[me], xs, xr, t // COLS, t % COLS).start()

        return 0

    lax.fori_loop(25, n, send_bulk, 0)
    lax.fori_loop(1, 25, lambda o, _: send_child(1, o), 0)
    y_ref[pl.ds(me, 1)] = x_ref[pl.ds(me, 1)]

    mi = jnp.concatenate(
        [maps(k)[k : k + 1, s * UR : (s + 1) * UR] for k in range(2) for s in range(ROWS)], axis=0
    )
    mj = jnp.concatenate(
        [maps(k)[k : k + 1, s * UCB : (s + 1) * UCB] for k in range(2) for s in range(COLS)], axis=0
    )
    child = iota((8, UR), 0) // ROWS

    def slots(hit, base):
        rank = dot_nn(hit.astype(F32).astype(BF16), before(hit.shape[1])).astype(jnp.int32)
        return jnp.where(hit, rank + base, -1)

    slot = slots((mi // RB) == r, 0)
    pslot = slots(mi < PW, CAPP * child)
    slot16 = slots((mj // CB) == c, CAPC * (iota((2 * COLS, UCB), 0) % COLS))
    eight = iota((8, 1), 0)
    row_of = []
    prow_of = []
    col_of = []
    for k in range(2):
        rows = []
        prows = []
        for s in range(ROWS):
            row = k * ROWS + s
            v = mi[row : row + 1, :]
            vals = jnp.where(eight == 0, (v % RB) // 256, v % 256).astype(F32).astype(BF16)
            got = dot_nt(vals, onehot(CAPR, slot[row : row + 1, :]))
            rows.append(got[0:1, :] * 256.0 + got[1:2, :])
            vals = jnp.broadcast_to((v % 256 + 1).astype(F32).astype(BF16), (8, UR))
            got = dot_nt(vals, onehot(2 * CAPP, pslot[row : row + 1, :]))
            prows.append(got[0:1, :] - 1.0)
        row_of.append(jnp.concatenate(rows, axis=1).astype(jnp.int32))
        prow_of.append(jnp.concatenate(prows, axis=1).astype(jnp.int32))
        tslot = jnp.concatenate(
            [slot16[k * COLS + s : k * COLS + s + 1, :] for s in range(COLS)], axis=1
        )
        v = (maps(k)[k : k + 1, :] % CB).astype(F32).astype(BF16)
        got = dot_nt(jnp.broadcast_to(v, (8, COLS * UCB)), onehot(COLS * CAPC, tslot))
        col_of.append(got[0:1, :].astype(jnp.int32))
    cpl = [onehot(CB, col_of[k]) for k in range(2)]

    def prepare():
        for k in range(2):
            for s in range(4):
                place_ref[k, s * 256 : (s + 1) * 256, :] = onehot(PW, row_of[k] - s * 256)
        e_ref[:, PW:] = (iota((PW, PW), 0) == iota((PW, PW), 1)).astype(F32)

    @pl.when(r != 0)
    def _():
        prepare()

    @pl.when(r == 0)
    def _():
        yp_ref[pl.ds(me, 1)] = xp_ref[pl.ds(c, 1)]
        remote(yp_ref.at[pl.ds(0, n - 1)], yp_ref.at[pl.ds(0, n - 1)], ps, prs, 1, c).wait_recv()
        total = f_ref[:PW, :]
        src = jnp.concatenate(
            [yp_ref[s * COLS : (s + 1) * COLS].reshape(COLS * CAPC, 2 * CAPP) for s in range(ROWS)],
            axis=1,
        )
        parts = parts3(src)
        for k in range(2):
            rpl = onehot(PW, prow_of[k])
            for part in parts:
                total = total + dot_nt(rpl, dot_nn(cpl[k], part).astype(BF16))
        xb_ref[...] = total

        @pl.when(c == 0)
        def _():
            pv_ref[0:16, :] = xb_ref[0:16, :]

            def piece(t, _):
                remote(
                    xb_ref.at[sixteenth(t)], pv_ref.at[sixteenth(t)], vs.at[0], vr.at[0],
                    t // 4, (t % 4) * 4,
                ).start()
                return 0

            lax.fori_loop(1, 16, piece, 0)

        def part_to(q, _):
            remote(
                xb_ref.at[quarter(q)], pr_ref.at[z, quarter(q)], qs, qr.at[z, q], y, q * 4 + z
            ).start()
            return 0

        @pl.when(y == 0)
        def _():
            pr_ref[pl.ds(z, 1), 0:64] = xb_ref[0:64, :].reshape(1, 64, CB)
            lax.fori_loop(1, 4, part_to, 0)

        @pl.when(y != 0)
        def _():
            lax.fori_loop(0, 4, part_to, 0)

        def half_to(i, h, row):
            remote(xb_ref.at[half(h)], xb_ref.at[half(h)], bs.at[i], br.at[h], row, c).start()

        half_to(0, 0, 1)
        half_to(1, 1, 3)
        half_to(2, 1, 1)
        half_to(3, 0, 3)

    mine = 4 * r + y

    @pl.when(z == 0)
    def _():
        @pl.when(mine != 0)
        def _():
            remote(pv_ref.at[sixteenth(mine)], pv_ref.at[sixteenth(mine)], vs.at[0], vr.at[0], r, c).wait_recv()

        for o in range(1, 4):
            remote(
                pv_ref.at[sixteenth(mine)], pv_ref.at[sixteenth(mine)], vt.at[o - 1], vr.at[0], r, y * 4 + o
            ).start()

    @pl.when(z != 0)
    def _():
        remote(pv_ref.at[sixteenth(mine)], pv_ref.at[sixteenth(mine)], vs.at[0], vr.at[0], r, c).wait_recv()

    def plane(o, _):
        t = lax.rem(mine + o, 16)
        remote(
            pv_ref.at[sixteenth(mine)], pv_ref.at[sixteenth(mine)], vs.at[1], vr.at[1],
            t // 4, (t % 4) * 4 + z,
        ).start()
        return 0

    lax.fori_loop(1, 16, plane, 0)

    @pl.when(jnp.logical_or(r != 0, me >= 4))
    def _():
        remote(pr_ref.at[z, quarter(y)], pr_ref.at[z, quarter(y)], qs, qr.at[z, y], r, c).wait_recv()

    def to_y(zz):
        for o in range(1, 4):
            remote(
                pr_ref.at[zz, quarter(y)], pr_ref.at[zz, quarter(y)], ds.at[2], qr.at[zz, y],
                r, lax.rem(y + o, 4) * 4 + z,
            ).start()

    for o in range(1, 4):
        remote(
            pr_ref.at[z, quarter(y)], pr_ref.at[z, quarter(y)], ds.at[1], qr.at[z, y],
            r, y * 4 + lax.rem(z + o, 4),
        ).start()
    to_y(z)

    @pl.when(r == 0)
    def _():
        prepare()

    for i in range(3):
        up = jnp.where(i >= z, i + 1, i)
        down = jnp.where(3 - i <= z, 2 - i, 3 - i)
        zz = jnp.where(z < 2, up, down)
        remote(pr_ref.at[zz, quarter(y)], pr_ref.at[zz, quarter(y)], qs, qr.at[zz, y], r, c).wait_recv()
        to_y(zz)

    @pl.when(r == 1)
    def _():
        remote(xb_ref.at[half(0)], xb_ref.at[half(0)], bs.at[0], br.at[0], r, c).wait_recv()
        remote(xb_ref.at[half(0)], xb_ref.at[half(0)], bs.at[0], br.at[0], 2, c).start()

    @pl.when(r == 3)
    def _():
        remote(xb_ref.at[half(1)], xb_ref.at[half(1)], bs.at[0], br.at[1], r, c).wait_recv()
        remote(xb_ref.at[half(1)], xb_ref.at[half(1)], bs.at[0], br.at[1], 2, c).start()

    remote(pv_ref.at[0:240], pv_ref.at[0:240], vs.at[1], vr.at[1], r, c).wait_recv()
    set_up(e_ref, pv_ref[...])
    eliminate(e_ref, 0, PW)
    inv = e_ref[:, PW:]

    @pl.when(c != 0)
    def _():
        remote(x_ref.at[pl.ds(0, n - 1)], y_ref.at[pl.ds(0, n - 1)], xs, xr, r, c).wait_recv()
        placed = []
        for k in range(2):
            src = jnp.concatenate(
                [y_ref[s * COLS : (s + 1) * COLS, k].reshape(COLS * CAPC, CAPR) for s in range(ROWS)],
                axis=1,
            )
            placed.append([dot_nn(cpl[k], part).astype(BF16) for part in split2(src)])
        for s in range(4):
            rows = slice(s * 256, (s + 1) * 256)
            total = f_ref[rows, :]
            for k in range(2):
                rpl = place_ref[k, rows, :]
                for w in placed[k]:
                    total = total + dot_nt(rpl, w)
            a_ref[rows, :] = total

    @pl.when(jnp.logical_or(r == 2, r == 3))
    def _():
        remote(xb_ref.at[half(0)], xb_ref.at[half(0)], bs.at[0], br.at[0], r, c).wait_recv()

    @pl.when(jnp.logical_or(r == 1, r == 2))
    def _():
        remote(xb_ref.at[half(1)], xb_ref.at[half(1)], bs.at[0], br.at[1], r, c).wait_recv()

    for zz in range(4):
        for o in range(1, 4):
            yy = lax.rem(y + o, 4)
            remote(
                pr_ref.at[zz, quarter(yy)], pr_ref.at[zz, quarter(yy)], qs, qr.at[zz, yy], r, c
            ).wait_recv()

    @pl.when(c == 0)
    def _():
        for s in range(4):
            o_ref[s * 256 : (s + 1) * 256, :] = lax.dot_general(
                pr_ref[s], inv, (((0,), (1,)), ((), ())), preferred_element_type=F32,
                precision=lax.Precision.HIGHEST,
            )

        @pl.when(r == 0)
        def _():
            o_ref[:PW, :] = e_ref[:, :PW].T

    @pl.when(c != 0)
    def _():
        right = dot3(dot_nn, inv, xb_ref[...])
        for s in range(4):
            rows = slice(s * 256, (s + 1) * 256)
            left = dot3(dot_nn, inv, pr_ref[s])
            o_ref[rows, :] = a_ref[rows, :] - dot3(dot_tn, left, right)

    @pl.when(c == 0)
    def _():
        remote(x_ref.at[0:60], y_ref.at[0:60], xs, xr, r, c).wait_send()

    @pl.when(c != 0)
    def _():
        remote(x_ref.at[0:59], y_ref.at[0:59], xs, xr, r, c).wait_send()

    remote(pv_ref.at[0:240], pv_ref.at[0:240], vs.at[1], vr.at[1], r, c).wait_send()
    remote(pr_ref.at[0, 0:192], pr_ref.at[0, 0:192], ds.at[1], br.at[0], r, c).wait_send()
    remote(pr_ref.at[0:3], pr_ref.at[0:3], ds.at[2], br.at[0], r, c).wait_send()

    @pl.when(z == 0)
    def _():
        for o in range(1, 4):
            remote(pv_ref.at[0:16], pv_ref.at[0:16], vt.at[o - 1], br.at[0], r, c).wait_send()

    @pl.when(r != 0)
    def _():
        remote(xp_ref, yp_ref.at[pl.ds(0, COLS)], ps, prs, r, c).wait_send()

    @pl.when(r == 0)
    def _():
        remote(xp_ref.at[0:15], yp_ref.at[0:15], ps, prs, r, c).wait_send()

        @pl.when(y == 0)
        def _():
            remote(xb_ref.at[0:192], xb_ref.at[0:192], qs, br.at[0], r, c).wait_send()

        @pl.when(y != 0)
        def _():
            remote(xb_ref, xb_ref, qs, br.at[0], r, c).wait_send()

        @pl.when(c == 0)
        def _():
            remote(xb_ref.at[0:240], xb_ref.at[0:240], vs.at[0], br.at[0], r, c).wait_send()

        for i in range(4):
            remote(xb_ref.at[0:128], xb_ref.at[0:128], bs.at[i], br.at[0], r, c).wait_send()

    @pl.when(jnp.logical_or(r == 1, r == 3))
    def _():
        remote(xb_ref.at[0:128], xb_ref.at[0:128], bs.at[0], br.at[0], r, c).wait_send()


def shape(*s):
    return jax.ShapeDtypeStruct(s, F32)


def per_device(front_matrix, child_updates, child_map):
    dma = pltpu.SemaphoreType.DMA
    out = pl.pallas_call(
        kernel,
        out_shape=shape(RB, CB),
        in_specs=[
            pl.BlockSpec(memory_space=pltpu.VMEM),
            pl.BlockSpec(memory_space=pltpu.VMEM),
            pl.BlockSpec(memory_space=pltpu.VMEM),
        ],
        out_specs=pl.BlockSpec(memory_space=pltpu.VMEM),
        scratch_shapes=[
            pltpu.VMEM((UR, UCB), F32),
            pltpu.VMEM((2, ROWS * UR), jnp.int32),
            pltpu.VMEM((2, RB, UR), BF16),
            pltpu.VMEM((RB, CB), F32),
            pltpu.VMEM((ROWS * COLS, 2, CAPC, CAPR), F32),
            pltpu.VMEM((ROWS * COLS, 2, CAPC, CAPR), F32),
            pltpu.VMEM((COLS, CAPC, 2 * CAPP), F32),
            pltpu.VMEM((ROWS * COLS, CAPC, 2 * CAPP), F32),
            pltpu.VMEM((PW, CB), F32),
            pltpu.VMEM((4, PW, CB), F32),
            pltpu.VMEM((PW, CB), F32),
            pltpu.VMEM((PW, 2 * PW), F32),
            dma((2,)), dma((2,)),
            dma, dma, dma, dma, dma((4,)), dma((2,)), dma, dma((4, 4)), dma((3,)), dma((2,)), dma((2,)),
            dma((3,)),
        ],
        compiler_params=pltpu.CompilerParams(
            vmem_limit_bytes=VMEM_LIMIT, collective_id=1, has_side_effects=True
        ),
    )(child_map[0], child_updates[0], front_matrix[0])
    zero = jnp.logical_and(lax.axis_index("row") == 0, lax.axis_index("col") > 0)
    kept = jnp.logical_or(iota((RB, CB), 0) >= PW, jnp.logical_not(zero))
    return jnp.where(kept, out, 0.0)[None]


def solution(mesh):
    in_specs = (P("front", "row", "col"), P("front", None, "row", "col"), P("front", None, None))
    return jax.shard_map(
        per_device, mesh=mesh, in_specs=in_specs, out_specs=P("front", "row", "col"), check_vma=False
    )
```
